32 devices in a mesh: ens: 2 (over y), lon: 8 (over z, x), lat: 2 (over core).
Axes of the slice: x: 2, y: 2, z: 4, core: 2. Of those that a mesh axis runs over, the one named last changes fastest.
Arguments:
- state_in: float32 [1024, 128, 256], P(('ens', 'lon'), 'lat'), parts along dimension 0, may hold values from -6 to 6
- diffusion: float32 [256], replicated, may hold values from 0.2 to 0.245
- conv_index: int32 [16, 2, 3072], P(('ens', 'lon'), 'lat'), parts along dimension 0, may hold values from 0 to 4095, as said below
- conv_count: int32 [2, 8, 2], P('ens', None, 'lat'), parts along dimension 0, may hold values from 8 to 3072, as said below
- w_first: bfloat16 [256, 1024], replicated, may hold values from -0.375 to 0.375
- w_hidden: bfloat16 [2, 1024, 1024], replicated, may hold values from -0.1875 to 0.1875
- w_last: bfloat16 [1024, 256], replicated, may hold values from -0.1875 to 0.1875
Outputs:
- state_out: float32 [1024, 128, 256], P(('ens', 'lon'), 'lat'), parts along dimension 0
The draws below stay inside these ranges and needn't reach their ends.
There are 2 independent parts, one for each index of `ens`. The reference program is written for one: setup_inputs(seed, part) draws one part's arguments, and reference() takes and returns one part's arrays. A program takes and returns all parts, laid end to end along the dimension named above; an argument that names none is the same for every part. Nothing has to cross between parts.
Inputs may be any that keep to these rules, and one draw needn't show every extreme that they name: `conv_index`: each device's list holds 3072 distinct local column numbers a * 64 + b for row a and place b of its block; only the first conv_count entries are convecting. `conv_count`: entry [0, l, m] counts the convecting columns of the device at lon index l and lat index m. Each count is a whole multiple of the number of lon devices, and the counts of one latitude band average exactly 1344.
All inputs are finite; a program needn't handle non-finite values.
Results may differ from the reference program's by a relative error of at most 0.0003.
Values may be sent and summed in bfloat16 or wider, within the bound.
A program may use at most 128 MiB of HBM per device.

```python
import jax
import jax.numpy as jnp
from jax import lax

HID = 1024
MIDDLE = 2
SWEEPS = 2
CLON = 64
CLAT = 64
FEAT = 256
LIST = 3072
MEANC = 1344
NLON = 512
NLAT = 128
N_LON = 8
N_LAT = 2


def band_counts(band_key):
    slot_depth = LIST // N_LON
    busy_key, order_key = jax.random.split(band_key)
    busiest = jax.random.randint(busy_key, (), 0, N_LON)
    shuffled = jax.random.permutation(order_key, (N_LON - 1) * (slot_depth - 1))
    chosen = (shuffled < MEANC - slot_depth - (N_LON - 1)).astype(jnp.int32)
    others = chosen.reshape(N_LON - 1, slot_depth - 1).sum(axis=1) + 1
    places = jnp.arange(N_LON, dtype=jnp.int32)
    other_slot = jnp.clip(places - (places > busiest).astype(jnp.int32), 0, N_LON - 2)
    return jnp.where(places == busiest, slot_depth, others[other_slot])


def draw_conv_count(key, part):
    key = jax.random.fold_in(key, 7)
    band_keys = jax.random.split(key, N_LAT)
    per_band = jax.vmap(band_counts)(band_keys)
    return (per_band.T * N_LON)[None].astype(jnp.int32)


def column_choice(column_key):
    return jax.random.permutation(column_key, CLON * CLAT)[:LIST].astype(jnp.int32)


def draw_conv_index(key, part):
    key = jax.random.fold_in(key, 11)
    device_keys = jax.random.split(key, N_LON * N_LAT)
    return jax.vmap(column_choice)(device_keys).reshape(N_LON, N_LAT, LIST)


def level_of(rng, dims, pieces, low, high):
    level, own = 1.0, jax.random.fold_in(rng, 6)
    for dim, blocks in pieces:
        draws = jnp.exp(jax.random.uniform(jax.random.fold_in(own, dim), (blocks,), jnp.float32, low / len(pieces), high / len(pieces)))
        level = level * jnp.repeat(draws, dims[dim] // blocks).reshape([-1 if axis == dim else 1 for axis in range(len(dims))])
    return level


def noise(rng, dims, width, limit, shards=(), kind=jnp.bfloat16):
    loudness = level_of(rng, dims, shards, -0.22, 0.18) if shards else 1.0
    values = jax.random.normal(rng, dims, jnp.float32) * width * loudness
    return jnp.minimum(jnp.maximum(values, -limit), limit).astype(kind)


def setup_inputs(seed: int = 0, part: int = 0) -> dict:
    splits = jax.random.split(jax.random.key(seed), 8)
    part_keys = jax.random.split(jax.random.fold_in(splits[7], part), 8)
    return {
        "state_in": noise(part_keys[0], (NLON, NLAT, FEAT), 1.0, 6.0, ((0, 8), (1, 2)), jnp.float32),
        "diffusion": jnp.clip(jax.random.uniform(splits[1], (FEAT,), jnp.float32, 0.2, 0.245), 0.2, 0.245),
        "conv_index": draw_conv_index(jax.random.fold_in(jax.random.fold_in(splits[7], part), 71), part),
        "conv_count": draw_conv_count(jax.random.fold_in(jax.random.fold_in(splits[7], part), 71), part),
        "w_first": noise(splits[4], (FEAT, HID), FEAT ** -0.5, 0.375),
        "w_hidden": noise(splits[5], (MIDDLE, HID, HID), HID ** -0.5, 0.1875),
        "w_last": noise(splits[6], (HID, FEAT), HID ** -0.5, 0.1875),
    }


def sweep_once(values, diffusion):
    east_west = jnp.roll(values, -1, 0) + jnp.roll(values, 1, 0)
    padded = jnp.pad(values, ((0, 0), (1, 1), (0, 0)))
    north_south = padded[:, 2:] + padded[:, :-2]
    return values + diffusion * (east_west + north_south - 4.0 * values)


def column_network(profile, w_first, w_hidden, w_last):
    hidden = jax.nn.silu(jnp.dot(profile, w_first, preferred_element_type=jnp.float32)).astype(jnp.bfloat16)
    for middle in range(w_hidden.shape[0]):
        hidden = jax.nn.silu(jnp.dot(hidden, w_hidden[middle], preferred_element_type=jnp.float32)).astype(jnp.bfloat16)
    return jnp.dot(hidden, w_last, preferred_element_type=jnp.float32).astype(jnp.bfloat16)


def reference(state_in, diffusion, conv_index, conv_count, w_first, w_hidden, w_last):
    before = state_in
    for repeat in range(SWEEPS):
        before = sweep_once(before, diffusion)
    counts = conv_count[0]
    places = jnp.arange(LIST, dtype=jnp.int32)
    listed = places[None, None, :] < counts[:, :, None]
    lon_start = (jnp.arange(N_LON, dtype=jnp.int32) * CLON)[:, None, None]
    lat_start = (jnp.arange(N_LAT, dtype=jnp.int32) * CLAT)[None, :, None]
    flat_rows = (lon_start + conv_index // CLAT) * NLAT + lat_start + conv_index % CLAT
    row_total = N_LON * N_LAT * MEANC
    padded_total = -(-row_total // 1024) * 1024
    (picked,) = jnp.nonzero(listed.reshape(-1), size=padded_total, fill_value=0)
    targets = flat_rows.reshape(-1)[picked]
    column_table = before.reshape(NLON * NLAT, FEAT)

    def tendency_block(block_rows):
        return column_network(column_table[block_rows].astype(jnp.bfloat16), w_first, w_hidden, w_last)

    tendency = lax.map(tendency_block, targets.reshape(-1, 1024)).reshape(-1, FEAT)[:row_total]
    after_physics = column_table.at[targets[:row_total]].add(tendency.astype(jnp.float32)).reshape(NLON, NLAT, FEAT)
    for repeat in range(SWEEPS):
        after_physics = sweep_once(after_physics, diffusion)
    return after_physics
```

```python
import functools

import jax
import jax.numpy as jnp
from jax import lax
from jax.experimental import pallas as pl
from jax.experimental.pallas import tpu as pltpu
from jax.sharding import PartitionSpec as P

HALO = 4
BLOCK = 8
PAD = 8
ALIGN = 16
TILE = 256
ROWS = 512


def silu(u):
    half = 0.5 * u
    return half + half * jnp.tanh(half)


def kernel(
    state, north, south, side, corner_n, corner_s, diffusion, keys, offs,
    w_first, w_hidden, w_last, out,
    a_buf, b_buf, packed, hid_a, hid_b, w1, wh, w3, in_sem, w_sem, out_sem,
):
    lon, lat, feat = state.shape
    lanes = feat // 2
    me = lax.axis_index("lat")
    own = pl.multiple_of(PAD + BLOCK * me, BLOCK)
    beside = pl.multiple_of(jnp.where(me == 0, PAD + lat, PAD), BLOCK)
    top, low = HALO, HALO + lon

    copies = []
    for half in range(2):
        cut = pl.ds(half * lanes, lanes)
        for source, row, rows, place, width in (
            (north, 0, HALO, own, lat),
            (south, low, HALO, own, lat),
            (side, top, lon, beside, BLOCK),
            (corner_n, 0, HALO, beside, BLOCK),
            (corner_s, low, HALO, beside, BLOCK),
            (state, top, lon, own, lat),
        ):
            copies.append(
                pltpu.make_async_copy(
                    source.at[:, :, cut],
                    a_buf.at[half, pl.ds(row, rows), pl.ds(place, width), :],
                    in_sem.at[len(copies)],
                )
            )
    weights = [
        pltpu.make_async_copy(w_first, w1, w_sem.at[0]),
        pltpu.make_async_copy(w_hidden, wh, w_sem.at[1]),
        pltpu.make_async_copy(w_last, w3, w_sem.at[2]),
    ]
    for copy in copies:
        copy.start()
    for copy in weights:
        copy.start()
    wide = a_buf.shape[2] - 2 * PAD

    def clear(row, carry):
        for buf in (a_buf, b_buf):
            for half in range(2):
                buf[half, row, 0:PAD, :] = jnp.zeros((PAD, lanes), jnp.float32)
                buf[half, row, PAD + wide :, :] = jnp.zeros((PAD, lanes), jnp.float32)
        return carry

    lax.fori_loop(0, a_buf.shape[1], clear, 0)
    for copy in copies:
        copy.wait()

    def sweep(src, dst, first, last):
        def row_step(row, carry):
            for half in range(2):
                amount = diffusion[0:1, half * lanes : (half + 1) * lanes]
                keep = 1.0 - 4.0 * amount
                here = src[half, row, PAD : PAD + wide, :]
                around = (
                    src[half, row - 1, PAD : PAD + wide, :]
                    + src[half, row + 1, PAD : PAD + wide, :]
                ) + (
                    src[half, row, PAD - 1 : PAD + wide - 1, :]
                    + src[half, row, PAD + 1 : PAD + wide + 1, :]
                )
                dst[half, row, PAD : PAD + wide, :] = keep * here + amount * around
            return carry

        lax.fori_loop(first, last, row_step, 0)

    sweep(a_buf, b_buf, 1, low + HALO - 1)
    sweep(b_buf, a_buf, 2, low + HALO - 2)

    per_tile = TILE // lat
    pieces = [
        [(HALO - 1, 1, beside, BLOCK), (low, 1, beside, BLOCK)],
        [(top, lon // 2, beside, BLOCK)],
        [(top + lon // 2, lon // 2, beside, BLOCK)],
        [(HALO - 2, 2, own, lat), (low, 2, own, lat)],
    ]
    n_side = len(pieces)
    n_main = lon // per_tile

    def select(tile, width):
        spot = lax.broadcasted_iota(jnp.int32, (TILE, width), 0).astype(jnp.float32)
        return jnp.where(spot == keys[pl.ds(tile, 1), 0:width], 1.0, 0.0).astype(jnp.bfloat16)

    def gather(tile, slices):
        halves = [
            jnp.concatenate(
                [
                    a_buf[half, pl.ds(row, rows), pl.ds(place, width), :].reshape(rows * width, lanes)
                    for row, rows, place, width in slices
                ],
                axis=0,
            ).astype(jnp.bfloat16)
            for half in range(2)
        ]
        values = jnp.concatenate(halves, axis=1)
        picked = jnp.dot(select(tile, values.shape[0]), values, preferred_element_type=jnp.float32)
        start = pl.multiple_of(offs[tile], ALIGN)
        packed[pl.ds(start, TILE), :] = picked.astype(jnp.bfloat16)

    def scatter(tile, slices):
        start = pl.multiple_of(offs[tile], ALIGN)
        change = packed[pl.ds(start, TILE), :]
        count = sum(rows * width for _, rows, _, width in slices)
        spread = lax.dot_general(
            select(tile, count), change, (((0,), (0,)), ((), ())), preferred_element_type=jnp.float32
        )
        for half in range(2):
            done = 0
            for row, rows, place, width in slices:
                part = spread[done : done + rows * width, half * lanes : (half + 1) * lanes]
                done += rows * width
                where = (half, pl.ds(row, rows), pl.ds(place, width), slice(None))
                a_buf[where] = a_buf[where] + part.reshape(rows, width, lanes)

    for tile, slices in enumerate(pieces):
        gather(tile, slices)

    def main_gather(step, carry):
        gather(n_side + step, [(top + per_tile * step, per_tile, own, lat)])
        return carry

    lax.fori_loop(0, n_main, main_gather, 0, unroll=2)
    for copy in weights:
        copy.wait()

    hidden = w1.shape[1]

    def layer(x, weight, dst):
        for column in range(0, hidden, TILE):
            u = jnp.dot(x, weight[:, column : column + TILE], preferred_element_type=jnp.float32)
            dst[:, column : column + TILE] = silu(u).astype(jnp.bfloat16)

    def network(step, carry):
        rows = pl.ds(pl.multiple_of(step * ROWS, ROWS), ROWS)
        layer(packed[rows, :], w1, hid_a)
        now, other = hid_a, hid_b
        for middle in range(wh.shape[0]):
            layer(now[...], wh.at[middle], other)
            now, other = other, now
        packed[rows, :] = jnp.dot(now[...], w3[...], preferred_element_type=jnp.float32).astype(
            jnp.bfloat16
        )
        return carry

    total = offs[n_side + n_main]
    lax.fori_loop(0, (total + ROWS - 1) // ROWS, network, 0)

    for tile, slices in enumerate(pieces):
        scatter(tile, slices)

    def main_scatter(step, carry):
        scatter(n_side + step, [(top + per_tile * step, per_tile, own, lat)])
        return carry

    lax.fori_loop(0, n_main, main_scatter, 0, unroll=2)

    sweep(a_buf, b_buf, 3, low + HALO - 3)
    parts = 4
    outs = []
    for part in range(parts):
        begin = part * lon // parts
        size = (part + 1) * lon // parts - begin
        sweep(b_buf, a_buf, top + begin, top + begin + size)
        for half in range(2):
            copy = pltpu.make_async_copy(
                a_buf.at[half, pl.ds(top + begin, size), pl.ds(own, lat), :],
                out.at[pl.ds(begin, size), :, pl.ds(half * lanes, lanes)],
                out_sem.at[len(outs)],
            )
            copy.start()
            outs.append(copy)
    for copy in outs:
        copy.wait()


def local(n_lon, n_lat, state_in, diffusion, conv_index, conv_count, w_first, w_hidden, w_last):
    lon, lat, feat = state_in.shape
    lat_place = lax.axis_index("lat")
    first_lat = lat_place == 0

    east = [(i, (i + 1) % n_lon) for i in range(n_lon)]
    west = [((i + 1) % n_lon, i) for i in range(n_lon)]
    swap = [(i, n_lat - 1 - i) for i in range(n_lat)]

    def across(pairs):
        return [(i * n_lat + k, j * n_lat + m) for i, j in pairs for k, m in swap]

    edge = jnp.where(first_lat, state_in[:, lat - BLOCK :], state_in[:, :BLOCK])
    north = lax.ppermute(state_in[lon - HALO :], "lon", east)
    south = lax.ppermute(state_in[:HALO], "lon", west)
    side = lax.ppermute(edge, "lat", swap)
    corner_n = lax.ppermute(edge[lon - HALO :], ("lon", "lat"), across(east))
    corner_s = lax.ppermute(edge[:HALO], ("lon", "lat"), across(west))

    listed = conv_index.reshape(-1)
    count = conv_count[0, lax.axis_index("lon"), 0]
    active = jnp.arange(listed.shape[0], dtype=jnp.int32) < count
    row_hot = (jnp.arange(lon, dtype=jnp.int32)[:, None] == (listed // lat)[None]) & active[None]
    place_hot = jnp.arange(lat, dtype=jnp.int32)[:, None] == (listed % lat)[None]
    mask = lax.dot_general(
        row_hot.astype(jnp.bfloat16), place_hot.astype(jnp.bfloat16), (((1,), (1,)), ((), ())),
        preferred_element_type=jnp.float32,
    )
    other = lax.ppermute(mask, "lat", swap)
    reach = jnp.arange(BLOCK)
    near = jnp.where(first_lat, other[:, :BLOCK], other[:, lat - BLOCK :])
    near = jnp.where(jnp.where(first_lat, reach < 2, reach >= BLOCK - 2)[None], near, 0.0)
    both = jnp.concatenate([mask, near], axis=1)
    above = lax.ppermute(both[lon - 2 :], "lon", east)
    below = lax.ppermute(both[:2], "lon", west)
    corner = jnp.concatenate([above[1, lat:], below[0, lat:]])
    tiles = jnp.concatenate(
        [
            jnp.pad(corner, (0, TILE - corner.shape[0]))[None],
            near.reshape(-1, TILE),
            jnp.concatenate([above[:, :lat], below[:, :lat]]).reshape(-1, TILE),
            mask.reshape(-1, TILE),
        ]
    )
    spots = jnp.arange(TILE)
    ranks = jnp.dot(
        tiles.astype(jnp.bfloat16),
        (spots[:, None] < spots[None]).astype(jnp.bfloat16),
        preferred_element_type=jnp.float32,
    )
    keys = jnp.where(tiles > 0.5, ranks, -1.0)
    counts = tiles.sum(axis=1).astype(jnp.int32)
    counts = (counts + ALIGN - 1) // ALIGN * ALIGN
    n_tiles = tiles.shape[0]
    order = jnp.arange(n_tiles + 1)
    offs = jnp.where(order[:n_tiles][None] < order[:, None], counts[None], 0).sum(axis=1)

    room = -(-(n_tiles * TILE + TILE) // ROWS) * ROWS
    wide = lat + BLOCK + 2 * PAD
    buf = pltpu.VMEM((2, lon + 2 * HALO, wide, feat // 2), jnp.float32)
    hidden = w_first.shape[1]
    anywhere = pl.BlockSpec(memory_space=pl.ANY)
    vmem = pl.BlockSpec(memory_space=pltpu.VMEM)
    smem = pl.BlockSpec(memory_space=pltpu.SMEM)
    return pl.pallas_call(
        kernel,
        out_shape=jax.ShapeDtypeStruct(state_in.shape, jnp.float32),
        in_specs=[anywhere] * 6 + [vmem, vmem, smem] + [anywhere] * 3,
        out_specs=anywhere,
        scratch_shapes=[
            buf,
            buf,
            pltpu.VMEM((room, feat), jnp.bfloat16),
            pltpu.VMEM((ROWS, hidden), jnp.bfloat16),
            pltpu.VMEM((ROWS, hidden), jnp.bfloat16),
            pltpu.VMEM(w_first.shape, jnp.bfloat16),
            pltpu.VMEM(w_hidden.shape, jnp.bfloat16),
            pltpu.VMEM(w_last.shape, jnp.bfloat16),
            pltpu.SemaphoreType.DMA((12,)),
            pltpu.SemaphoreType.DMA((3,)),
            pltpu.SemaphoreType.DMA((8,)),
        ],
        compiler_params=pltpu.CompilerParams(vmem_limit_bytes=50 * 1024 * 1024),
    )(
        state_in, north, south, side, corner_n, corner_s, diffusion[None], keys, offs,
        w_first, w_hidden, w_last,
    )


def solution(mesh):
    return jax.shard_map(
        functools.partial(local, mesh.shape["lon"], mesh.shape["lat"]),
        mesh=mesh,
        in_specs=(
            P(("ens", "lon"), "lat", None),
            P(),
            P(("ens", "lon"), "lat", None),
            P("ens", None, "lat"),
            P(),
            P(),
            P(),
        ),
        out_specs=P(("ens", "lon"), "lat", None),
        check_vma=False,
    )
```

```python
import functools

import jax
import jax.numpy as jnp
from jax import lax
from jax.experimental import pallas as pl
from jax.experimental.pallas import tpu as pltpu
from jax.sharding import PartitionSpec as P

HALO = 4
BLOCK = 8
PAD = 8
ALIGN = 16
TILE = 256
ROWS = 512
LANES = 128


def silu(u):
    half = 0.5 * u
    return half + half * jnp.tanh(half)


def kernel(
    state, north, south, side, corner_n, corner_s, diffusion, keys, offs,
    w_first, w_hidden, w_last, out,
    a_buf, b_buf, packed, hid_a, hid_b, w1, wh, w3, rows_in, in_sem, w_sem, out_sem,
):
    lon, lat, feat = state.shape
    lanes = feat // 2
    me = lax.axis_index("lat")
    own = pl.multiple_of(PAD + BLOCK * me, BLOCK)
    beside = pl.multiple_of(jnp.where(me == 0, PAD + lat, PAD), BLOCK)
    top, low = HALO, HALO + lon

    copies = []
    for half in range(2):
        cut = pl.ds(half * lanes, lanes)
        for source, row, rows, place, width in (
            (side, top, lon, beside, BLOCK),
            (corner_n, 0, HALO, beside, BLOCK),
            (corner_s, low, HALO, beside, BLOCK),
            (state, top, lon, own, lat),
        ):
            copies.append(
                pltpu.make_async_copy(
                    source.at[:, :, cut],
                    a_buf.at[half, pl.ds(row, rows), pl.ds(place, width), :],
                    in_sem.at[len(copies)],
                )
            )
    for source, which in ((north, 0), (south, 1)):
        copies.append(pltpu.make_async_copy(source, rows_in.at[which], in_sem.at[len(copies)]))
    weights = [
        pltpu.make_async_copy(w_first, w1, w_sem.at[0]),
        pltpu.make_async_copy(w_hidden, wh, w_sem.at[1]),
        pltpu.make_async_copy(w_last, w3, w_sem.at[2]),
    ]
    for copy in copies:
        copy.start()
    for copy in weights:
        copy.start()
    wide = a_buf.shape[2] - 2 * PAD

    def clear(row, carry):
        for buf in (a_buf, b_buf):
            for half in range(2):
                buf[half, row, 0:PAD, :] = jnp.zeros((PAD, lanes), jnp.float32)
                buf[half, row, PAD + wide :, :] = jnp.zeros((PAD, lanes), jnp.float32)
        return carry

    lax.fori_loop(0, a_buf.shape[1], clear, 0)
    for copy in copies:
        copy.wait()
    for which, row in ((0, 0), (1, low)):
        for half in range(2):
            cells = rows_in[which, :, :, half * lanes : (half + 1) * lanes].astype(jnp.float32)
            a_buf[half, row : row + HALO, pl.ds(own, lat), :] = cells

    def sweep(src, dst, first, last):
        def row_step(row, carry):
            for half in range(2):
                amount = diffusion[0:1, half * lanes : (half + 1) * lanes]
                keep = 1.0 - 4.0 * amount
                here = src[half, row, PAD : PAD + wide, :]
                around = (
                    src[half, row - 1, PAD : PAD + wide, :]
                    + src[half, row + 1, PAD : PAD + wide, :]
                ) + (
                    src[half, row, PAD - 1 : PAD + wide - 1, :]
                    + src[half, row, PAD + 1 : PAD + wide + 1, :]
                )
                dst[half, row, PAD : PAD + wide, :] = keep * here + amount * around
            return carry

        lax.fori_loop(first, last, row_step, 0)

    sweep(a_buf, b_buf, 1, low + HALO - 1)
    sweep(b_buf, a_buf, 2, low + HALO - 2)

    per_tile = TILE // lat
    pieces = [
        [(HALO - 1, 1, beside, BLOCK), (low, 1, beside, BLOCK)],
        [(top, lon // 2, beside, BLOCK)],
        [(top + lon // 2, lon // 2, beside, BLOCK)],
        [(HALO - 2, 2, own, lat), (low, 2, own, lat)],
    ]
    n_side = len(pieces)
    n_main = lon // per_tile

    def select(tile, width):
        spot = lax.broadcasted_iota(jnp.int32, (TILE, width), 0).astype(jnp.float32)
        return jnp.where(spot == keys[pl.ds(tile, 1), 0:width], 1.0, 0.0).astype(jnp.bfloat16)

    def gather(tile, slices):
        halves = [
            jnp.concatenate(
                [
                    a_buf[half, pl.ds(row, rows), pl.ds(place, width), :].reshape(rows * width, lanes)
                    for row, rows, place, width in slices
                ],
                axis=0,
            ).astype(jnp.bfloat16)
            for half in range(2)
        ]
        values = jnp.concatenate(halves, axis=1)
        picked = jnp.dot(select(tile, values.shape[0]), values, preferred_element_type=jnp.float32)
        start = pl.multiple_of(offs[tile], ALIGN)
        packed[pl.ds(start, TILE), :] = picked.astype(jnp.bfloat16)

    def scatter(tile, slices):
        start = pl.multiple_of(offs[tile], ALIGN)
        change = packed[pl.ds(start, TILE), :]
        count = sum(rows * width for _, rows, _, width in slices)
        spread = lax.dot_general(
            select(tile, count), change, (((0,), (0,)), ((), ())), preferred_element_type=jnp.float32
        )
        for half in range(2):
            done = 0
            for row, rows, place, width in slices:
                part = spread[done : done + rows * width, half * lanes : (half + 1) * lanes]
                done += rows * width
                where = (half, pl.ds(row, rows), pl.ds(place, width), slice(None))
                a_buf[where] = a_buf[where] + part.reshape(rows, width, lanes)

    for tile, slices in enumerate(pieces):
        gather(tile, slices)

    def main_gather(step, carry):
        gather(n_side + step, [(top + per_tile * step, per_tile, own, lat)])
        return carry

    lax.fori_loop(0, n_main, main_gather, 0, unroll=2)
    for copy in weights:
        copy.wait()

    hidden = w1.shape[1]

    def layer(x, weight, dst):
        for column in range(0, hidden, TILE):
            u = jnp.dot(x, weight[:, column : column + TILE], preferred_element_type=jnp.float32)
            dst[:, column : column + TILE] = silu(u).astype(jnp.bfloat16)

    def network(step, carry):
        rows = pl.ds(pl.multiple_of(step * ROWS, ROWS), ROWS)
        layer(packed[rows, :], w1, hid_a)
        now, other = hid_a, hid_b
        for middle in range(wh.shape[0]):
            layer(now[...], wh.at[middle], other)
            now, other = other, now
        packed[rows, :] = jnp.dot(now[...], w3[...], preferred_element_type=jnp.float32).astype(
            jnp.bfloat16
        )
        return carry

    total = offs[n_side + n_main]
    lax.fori_loop(0, (total + ROWS - 1) // ROWS, network, 0)

    for tile, slices in enumerate(pieces):
        scatter(tile, slices)

    def main_scatter(step, carry):
        scatter(n_side + step, [(top + per_tile * step, per_tile, own, lat)])
        return carry

    lax.fori_loop(0, n_main, main_scatter, 0, unroll=2)

    sweep(a_buf, b_buf, 3, low + HALO - 3)
    parts = 4
    outs = []
    for part in range(parts):
        begin = part * lon // parts
        size = (part + 1) * lon // parts - begin
        sweep(b_buf, a_buf, top + begin, top + begin + size)
        for half in range(2):
            copy = pltpu.make_async_copy(
                a_buf.at[half, pl.ds(top + begin, size), pl.ds(own, lat), :],
                out.at[pl.ds(begin, size), :, pl.ds(half * lanes, lanes)],
                out_sem.at[len(outs)],
            )
            copy.start()
            outs.append(copy)
    for copy in outs:
        copy.wait()


def exchange(
    n_lon, state, listed, counts,
    north, south, side, corner_n, corner_s, mask, other, above, below, above_x, below_x,
    edges, lines, edge_sem, send_sem, recv_sem,
):
    lon, lat, _ = state.shape
    place, me = lax.axis_index("lon"), lax.axis_index("lat")
    east, west, across = lax.rem(place + 1, n_lon), lax.rem(place + n_lon - 1, n_lon), 1 - me
    others = [(west, me), (east, me), (place, across), (west, across), (east, across)]

    def device(spot):
        return {"lon": spot[0], "lat": spot[1]}

    loads = [
        pltpu.make_async_copy(state.at[pl.ds(row, HALO)], edges.at[which], edge_sem.at[which])
        for which, row in ((0, 0), (1, lon - HALO))
    ]
    for load in loads:
        load.start()
    barrier = pltpu.get_barrier_semaphore()
    for spot in others:
        pl.semaphore_signal(
            barrier, inc=1, device_id=device(spot), device_id_type=pl.DeviceIdType.MESH
        )
    pl.semaphore_wait(barrier, len(others))

    sent = []

    def send(source, target, spot):
        copy = pltpu.make_async_remote_copy(
            src_ref=source,
            dst_ref=target,
            send_sem=send_sem.at[len(sent)],
            recv_sem=recv_sem.at[len(sent)],
            device_id=device(spot),
            device_id_type=pl.DeviceIdType.MESH,
        )
        copy.start()
        sent.append(copy)

    for which, target, spot in ((0, south, others[0]), (1, north, others[1])):
        loads[which].wait()
        lines[which] = edges[which].astype(jnp.bfloat16)
        send(lines.at[which], target, spot)
    cut = pl.ds(pl.multiple_of(jnp.where(me == 0, lat - BLOCK, 0), BLOCK), BLOCK)
    send(state.at[pl.ds(0, HALO), cut], corner_s, others[3])
    send(state.at[pl.ds(lon - HALO, HALO), cut], corner_n, others[4])
    send(state.at[:, cut], side, others[2])

    numbers = listed[...]
    length = numbers.shape[1]
    active = lax.broadcasted_iota(jnp.int32, (1, length), 1) < counts[place]
    rows = jnp.where(active, lax.shift_right_logical(numbers, jnp.int32(lat.bit_length() - 1)), -1)
    spots = numbers & (lat - 1)
    row_hot = jnp.where(lax.broadcasted_iota(jnp.int32, (lon, length), 0) == rows, 1.0, 0.0)
    spot_hot = jnp.where(lax.broadcasted_iota(jnp.int32, (LANES, length), 0) == spots, 1.0, 0.0)
    mask[...] = lax.dot_general(
        row_hot.astype(jnp.bfloat16), spot_hot.astype(jnp.bfloat16), (((1,), (1,)), ((), ())),
        preferred_element_type=jnp.float32,
    )
    first, last = mask.at[pl.ds(0, BLOCK)], mask.at[pl.ds(lon - BLOCK, BLOCK)]
    send(mask, other, others[2])
    send(first, below, others[0])
    send(last, above, others[1])
    send(first, below_x, others[3])
    send(last, above_x, others[4])
    for copy in sent:
        copy.wait()


def take_near(rows, lat, first_lat):
    reach = jnp.arange(BLOCK)
    near = jnp.where(first_lat, rows[:, :BLOCK], rows[:, lat - BLOCK : lat])
    return jnp.where(jnp.where(first_lat, reach < 2, reach >= BLOCK - 2)[None], near, 0.0)


def local(n_lon, state_in, diffusion, conv_index, conv_count, w_first, w_hidden, w_last):
    lon, lat, feat = state_in.shape
    lat_place = lax.axis_index("lat")
    first_lat = lat_place == 0

    listed = conv_index.reshape(1, -1)
    anywhere = pl.BlockSpec(memory_space=pl.ANY)
    vmem = pl.BlockSpec(memory_space=pltpu.VMEM)
    smem = pl.BlockSpec(memory_space=pltpu.SMEM)
    shape = jax.ShapeDtypeStruct
    lines = shape((HALO, lat, feat), jnp.bfloat16)
    block = shape((HALO, BLOCK, feat), jnp.float32)
    few = shape((BLOCK, LANES), jnp.float32)
    full = shape((lon, LANES), jnp.float32)
    north, south, side, corner_n, corner_s, mask, other, above, below, above_x, below_x = pl.pallas_call(
        functools.partial(exchange, n_lon),
        out_shape=(lines, lines, shape((lon, BLOCK, feat), jnp.float32), block, block)
        + (full, full, few, few, few, few),
        in_specs=[anywhere, vmem, smem],
        out_specs=(anywhere,) * 5 + (vmem,) * 6,
        scratch_shapes=[
            pltpu.VMEM((2, HALO, lat, feat), jnp.float32),
            pltpu.VMEM((2, HALO, lat, feat), jnp.bfloat16),
            pltpu.SemaphoreType.DMA((2,)),
            pltpu.SemaphoreType.DMA((10,)),
            pltpu.SemaphoreType.DMA((10,)),
        ],
        compiler_params=pltpu.CompilerParams(collective_id=0, has_side_effects=True),
    )(state_in, listed, conv_count[0, :, 0])
    mask = mask[:, :lat]
    other = other[:, :lat]
    above = jnp.concatenate([above[BLOCK - 2 :, :lat], take_near(above_x[BLOCK - 2 :], lat, first_lat)], axis=1)
    below = jnp.concatenate([below[:2, :lat], take_near(below_x[:2], lat, first_lat)], axis=1)
    near = take_near(other, lat, first_lat)
    corner = jnp.concatenate([above[1, lat:], below[0, lat:]])
    tiles = jnp.concatenate(
        [
            jnp.pad(corner, (0, TILE - corner.shape[0]))[None],
            near.reshape(-1, TILE),
            jnp.concatenate([above[:, :lat], below[:, :lat]]).reshape(-1, TILE),
            mask.reshape(-1, TILE),
        ]
    )
    spots = jnp.arange(TILE)
    ranks = jnp.dot(
        tiles.astype(jnp.bfloat16),
        (spots[:, None] < spots[None]).astype(jnp.bfloat16),
        preferred_element_type=jnp.float32,
    )
    keys = jnp.where(tiles > 0.5, ranks, -1.0)
    counts = tiles.sum(axis=1).astype(jnp.int32)
    counts = (counts + ALIGN - 1) // ALIGN * ALIGN
    n_tiles = tiles.shape[0]
    order = jnp.arange(n_tiles + 1)
    offs = jnp.where(order[:n_tiles][None] < order[:, None], counts[None], 0).sum(axis=1)

    room = -(-(n_tiles * TILE + TILE) // ROWS) * ROWS
    wide = lat + BLOCK + 2 * PAD
    buf = pltpu.VMEM((2, lon + 2 * HALO, wide, feat // 2), jnp.float32)
    hidden = w_first.shape[1]
    return pl.pallas_call(
        kernel,
        out_shape=jax.ShapeDtypeStruct(state_in.shape, jnp.float32),
        in_specs=[anywhere] * 6 + [vmem, vmem, smem] + [anywhere] * 3,
        out_specs=anywhere,
        scratch_shapes=[
            buf,
            buf,
            pltpu.VMEM((room, feat), jnp.bfloat16),
            pltpu.VMEM((ROWS, hidden), jnp.bfloat16),
            pltpu.VMEM((ROWS, hidden), jnp.bfloat16),
            pltpu.VMEM(w_first.shape, jnp.bfloat16),
            pltpu.VMEM(w_hidden.shape, jnp.bfloat16),
            pltpu.VMEM(w_last.shape, jnp.bfloat16),
            pltpu.VMEM((2,) + north.shape, jnp.bfloat16),
            pltpu.SemaphoreType.DMA((10,)),
            pltpu.SemaphoreType.DMA((3,)),
            pltpu.SemaphoreType.DMA((8,)),
        ],
        compiler_params=pltpu.CompilerParams(vmem_limit_bytes=50 * 1024 * 1024),
    )(
        state_in, north, south, side, corner_n, corner_s, diffusion[None], keys, offs,
        w_first, w_hidden, w_last,
    )


def solution(mesh):
    return jax.shard_map(
        functools.partial(local, mesh.shape["lon"]),
        mesh=mesh,
        in_specs=(
            P(("ens", "lon"), "lat", None),
            P(),
            P(("ens", "lon"), "lat", None),
            P("ens", None, "lat"),
            P(),
            P(),
            P(),
        ),
        out_specs=P(("ens", "lon"), "lat", None),
        check_vma=False,
    )
```

```python
import functools

import jax
import jax.numpy as jnp
from jax import lax
from jax.experimental import pallas as pl
from jax.experimental.pallas import tpu as pltpu
from jax.sharding import PartitionSpec as P

HALO = 4
BLOCK = 8
PAD = 8
ALIGN = 16
TILE = 256
ROWS = 512


def silu(u):
    half = 0.5 * u
    return half + half * jnp.tanh(half)


def kernel(
    state, north, south, side, corner_n, corner_s, diffusion, keys, offs,
    w_first, w_hidden, w_last, out,
    a_buf, b_buf, packed, hid_a, hid_b, w1, wh, w3, rows_in, in_sem, w_sem, out_sem,
):
    lon, lat, feat = state.shape
    lanes = feat // 2
    me = lax.axis_index("lat")
    own = pl.multiple_of(PAD + BLOCK * me, BLOCK)
    beside = pl.multiple_of(jnp.where(me == 0, PAD + lat, PAD), BLOCK)
    top, low = HALO, HALO + lon

    copies = []
    for half in range(2):
        cut = pl.ds(half * lanes, lanes)
        for source, row, rows, place, width in (
            (side, top, lon, beside, BLOCK),
            (corner_n, 0, HALO, beside, BLOCK),
            (corner_s, low, HALO, beside, BLOCK),
            (state, top, lon, own, lat),
        ):
            copies.append(
                pltpu.make_async_copy(
                    source.at[:, :, cut],
                    a_buf.at[half, pl.ds(row, rows), pl.ds(place, width), :],
                    in_sem.at[len(copies)],
                )
            )
    for source, which in ((north, 0), (south, 1)):
        copies.append(pltpu.make_async_copy(source, rows_in.at[which], in_sem.at[len(copies)]))
    weights = [
        pltpu.make_async_copy(w_first, w1, w_sem.at[0]),
        pltpu.make_async_copy(w_hidden, wh, w_sem.at[1]),
        pltpu.make_async_copy(w_last, w3, w_sem.at[2]),
    ]
    for copy in copies:
        copy.start()
    for copy in weights:
        copy.start()
    wide = a_buf.shape[2] - 2 * PAD

    def clear(row, carry):
        for buf in (a_buf, b_buf):
            for half in range(2):
                buf[half, row, 0:PAD, :] = jnp.zeros((PAD, lanes), jnp.float32)
                buf[half, row, PAD + wide :, :] = jnp.zeros((PAD, lanes), jnp.float32)
        return carry

    lax.fori_loop(0, a_buf.shape[1], clear, 0)
    for copy in copies:
        copy.wait()
    for which, row in ((0, 0), (1, low)):
        for half in range(2):
            cells = rows_in[which, :, :, half * lanes : (half + 1) * lanes].astype(jnp.float32)
            a_buf[half, row : row + HALO, pl.ds(own, lat), :] = cells

    def sweep(src, dst, first, last):
        def row_step(row, carry):
            for half in range(2):
                amount = diffusion[0:1, half * lanes : (half + 1) * lanes]
                keep = 1.0 - 4.0 * amount
                here = src[half, row, PAD : PAD + wide, :]
                around = (
                    src[half, row - 1, PAD : PAD + wide, :]
                    + src[half, row + 1, PAD : PAD + wide, :]
                ) + (
                    src[half, row, PAD - 1 : PAD + wide - 1, :]
                    + src[half, row, PAD + 1 : PAD + wide + 1, :]
                )
                dst[half, row, PAD : PAD + wide, :] = keep * here + amount * around
            return carry

        lax.fori_loop(first, last, row_step, 0, unroll=2)

    sweep(a_buf, b_buf, 1, low + HALO - 1)
    sweep(b_buf, a_buf, 2, low + HALO - 2)

    per_tile = TILE // lat
    pieces = [
        [(HALO - 1, 1, beside, BLOCK), (low, 1, beside, BLOCK)],
        [(top, lon // 2, beside, BLOCK)],
        [(top + lon // 2, lon // 2, beside, BLOCK)],
        [(HALO - 2, 2, own, lat), (low, 2, own, lat)],
    ]
    n_side = len(pieces)
    n_main = lon // per_tile

    def select(tile, width):
        spot = lax.broadcasted_iota(jnp.int32, (TILE, width), 0).astype(jnp.float32)
        return jnp.where(spot == keys[pl.ds(tile, 1), 0:width], 1.0, 0.0).astype(jnp.bfloat16)

    def gather(tile, slices):
        halves = [
            jnp.concatenate(
                [
                    a_buf[half, pl.ds(row, rows), pl.ds(place, width), :].reshape(rows * width, lanes)
                    for row, rows, place, width in slices
                ],
                axis=0,
            ).astype(jnp.bfloat16)
            for half in range(2)
        ]
        values = jnp.concatenate(halves, axis=1)
        picked = jnp.dot(select(tile, values.shape[0]), values, preferred_element_type=jnp.float32)
        start = pl.multiple_of(offs[tile], ALIGN)
        packed[pl.ds(start, TILE), :] = picked.astype(jnp.bfloat16)

    def scatter(tile, slices):
        start = pl.multiple_of(offs[tile], ALIGN)
        change = packed[pl.ds(start, TILE), :]
        count = sum(rows * width for _, rows, _, width in slices)
        spread = lax.dot_general(
            select(tile, count), change, (((0,), (0,)), ((), ())), preferred_element_type=jnp.float32
        )
        for half in range(2):
            done = 0
            for row, rows, place, width in slices:
                part = spread[done : done + rows * width, half * lanes : (half + 1) * lanes]
                done += rows * width
                where = (half, pl.ds(row, rows), pl.ds(place, width), slice(None))
                a_buf[where] = a_buf[where] + part.reshape(rows, width, lanes)

    for tile, slices in enumerate(pieces):
        gather(tile, slices)

    def main_gather(step, carry):
        gather(n_side + step, [(top + per_tile * step, per_tile, own, lat)])
        return carry

    lax.fori_loop(0, n_main, main_gather, 0, unroll=2)
    for copy in weights:
        copy.wait()

    hidden = w1.shape[1]

    def layer(x, weight, dst):
        for column in range(0, hidden, TILE):
            u = jnp.dot(x, weight[:, column : column + TILE], preferred_element_type=jnp.float32)
            dst[:, column : column + TILE] = silu(u).astype(jnp.bfloat16)

    def network(step, carry):
        rows = pl.ds(pl.multiple_of(step * ROWS, ROWS), ROWS)
        layer(packed[rows, :], w1, hid_a)
        now, other = hid_a, hid_b
        for middle in range(wh.shape[0]):
            layer(now[...], wh.at[middle], other)
            now, other = other, now
        packed[rows, :] = jnp.dot(now[...], w3[...], preferred_element_type=jnp.float32).astype(
            jnp.bfloat16
        )
        return carry

    total = offs[n_side + n_main]
    lax.fori_loop(0, (total + ROWS - 1) // ROWS, network, 0)

    for tile, slices in enumerate(pieces):
        scatter(tile, slices)

    def main_scatter(step, carry):
        scatter(n_side + step, [(top + per_tile * step, per_tile, own, lat)])
        return carry

    lax.fori_loop(0, n_main, main_scatter, 0, unroll=2)

    sweep(a_buf, b_buf, 3, low + HALO - 3)
    parts = 4
    outs = []
    for part in range(parts):
        begin = part * lon // parts
        size = (part + 1) * lon // parts - begin
        sweep(b_buf, a_buf, top + begin, top + begin + size)
        for half in range(2):
            copy = pltpu.make_async_copy(
                a_buf.at[half, pl.ds(top + begin, size), pl.ds(own, lat), :],
                out.at[pl.ds(begin, size), :, pl.ds(half * lanes, lanes)],
                out_sem.at[len(outs)],
            )
            copy.start()
            outs.append(copy)
    for copy in outs:
        copy.wait()


def exchange(
    n_lon, state, listed, counts,
    north, south, side, corner_n, corner_s, tiles,
    mine, strip, above, below, other, above_x, below_x, edges, lines, edge_sem, send_sem, recv_sem,
):
    lon, lat, _ = state.shape
    place, me = lax.axis_index("lon"), lax.axis_index("lat")
    east, west, across = lax.rem(place + 1, n_lon), lax.rem(place + n_lon - 1, n_lon), 1 - me
    others = [(west, me), (east, me), (place, across), (west, across), (east, across)]

    def device(spot):
        return {"lon": spot[0], "lat": spot[1]}

    loads = [
        pltpu.make_async_copy(state.at[pl.ds(row, HALO)], edges.at[which], edge_sem.at[which])
        for which, row in ((0, 0), (1, lon - HALO))
    ]
    for load in loads:
        load.start()
    barrier = pltpu.get_barrier_semaphore()
    for spot in others:
        pl.semaphore_signal(
            barrier, inc=1, device_id=device(spot), device_id_type=pl.DeviceIdType.MESH
        )
    pl.semaphore_wait(barrier, len(others))

    sent = []

    def send(source, target, spot):
        copy = pltpu.make_async_remote_copy(
            src_ref=source,
            dst_ref=target,
            send_sem=send_sem.at[len(sent)],
            recv_sem=recv_sem.at[len(sent)],
            device_id=device(spot),
            device_id_type=pl.DeviceIdType.MESH,
        )
        copy.start()
        sent.append(copy)

    for which, target, spot in ((0, south, others[0]), (1, north, others[1])):
        loads[which].wait()
        lines[which] = edges[which].astype(jnp.bfloat16)
        send(lines.at[which], target, spot)
    cut = pl.ds(pl.multiple_of(jnp.where(me == 0, lat - BLOCK, 0), BLOCK), BLOCK)
    send(state.at[pl.ds(0, HALO), cut], corner_s, others[3])
    send(state.at[pl.ds(lon - HALO, HALO), cut], corner_n, others[4])
    send(state.at[:, cut], side, others[2])

    numbers = listed[...]
    length = numbers.shape[1]
    active = lax.broadcasted_iota(jnp.int32, (1, length), 1) < counts[place]
    numbers = jnp.where(active, numbers, -1)
    rows = lax.shift_right_arithmetic(numbers, jnp.int32(lat.bit_length() - 1))
    spots = numbers & (lat - 1)

    def hot(number, size):
        same = lax.broadcasted_iota(jnp.int32, (size, length), 0) == number
        return jnp.where(same, 1.0, 0.0).astype(jnp.bfloat16)

    def marks(tile, position, size):
        return lax.dot_general(
            hot(tile, size), hot(position, TILE), (((1,), (1,)), ((), ())),
            preferred_element_type=jnp.float32,
        )

    n_main = lon * lat // TILE
    mine[...] = marks(
        lax.shift_right_arithmetic(numbers, jnp.int32(TILE.bit_length() - 1)), numbers & (TILE - 1), n_main
    )
    height = TILE // BLOCK
    reached = jnp.where(me == 0, lat - 2, 0)
    close = (spots >= reached) & (spots < reached + 2)
    strip_tile = jnp.where(
        close, lax.shift_right_arithmetic(rows, jnp.int32(height.bit_length() - 1)), -1
    )
    strip[...] = marks(strip_tile, (rows & (height - 1)) * BLOCK + (spots & (BLOCK - 1)), BLOCK)
    send(mine.at[pl.ds(0, BLOCK)], below, others[0])
    send(mine.at[pl.ds(n_main - BLOCK, BLOCK)], above, others[1])
    send(strip, below_x, others[3])
    send(strip, above_x, others[4])
    send(strip, other, others[2])
    for copy in sent:
        copy.wait()

    n_strip = lon // height
    lane = lax.broadcasted_iota(jnp.int32, (BLOCK, TILE), 1)
    from_n = pltpu.roll(above_x[...], BLOCK, 1)[n_strip - 1 : n_strip]
    from_s = pltpu.roll(below_x[...], BLOCK, 1)[0:1]
    lane = lane[0:1]
    tiles[0:1, :] = jnp.where(lane < BLOCK, from_n, jnp.where(lane < 2 * BLOCK, from_s, 0.0))
    tiles[1 : 1 + n_strip, :] = other[0:n_strip, :]
    near = 2 * lat
    tiles[1 + n_strip : 2 + n_strip, 0:near] = above[BLOCK - 1 : BLOCK, TILE - near :]
    tiles[1 + n_strip : 2 + n_strip, near:] = below[0:1, 0:near]
    tiles[2 + n_strip :, :] = mine[...]


def local(n_lon, state_in, diffusion, conv_index, conv_count, w_first, w_hidden, w_last):
    lon, lat, feat = state_in.shape

    listed = conv_index.reshape(1, -1)
    anywhere = pl.BlockSpec(memory_space=pltpu.HBM)
    vmem = pl.BlockSpec(memory_space=pltpu.VMEM)
    smem = pl.BlockSpec(memory_space=pltpu.SMEM)
    shape = jax.ShapeDtypeStruct
    lines = shape((HALO, lat, feat), jnp.bfloat16)
    block = shape((HALO, BLOCK, feat), jnp.float32)
    n_tiles = 2 + lon * BLOCK // TILE + lon * lat // TILE
    few = pltpu.VMEM((BLOCK, TILE), jnp.float32)
    north, south, side, corner_n, corner_s, tiles = pl.pallas_call(
        functools.partial(exchange, n_lon),
        out_shape=(lines, lines, shape((lon, BLOCK, feat), jnp.float32), block, block)
        + (shape((n_tiles, TILE), jnp.float32),),
        in_specs=[anywhere, vmem, smem],
        out_specs=(anywhere,) * 5 + (vmem,),
        scratch_shapes=[
            pltpu.VMEM((lon * lat // TILE, TILE), jnp.float32),
            few, few, few, few, few, few,
            pltpu.VMEM((2, HALO, lat, feat), jnp.float32),
            pltpu.VMEM((2, HALO, lat, feat), jnp.bfloat16),
            pltpu.SemaphoreType.DMA((2,)),
            pltpu.SemaphoreType.DMA((10,)),
            pltpu.SemaphoreType.DMA((10,)),
        ],
        compiler_params=pltpu.CompilerParams(
            collective_id=0, has_side_effects=True, vmem_limit_bytes=60 * 1024 * 1024
        ),
    )(state_in, listed, conv_count[0, :, 0])
    spots = jnp.arange(TILE)
    ranks = jnp.dot(
        tiles.astype(jnp.bfloat16),
        (spots[:, None] < spots[None]).astype(jnp.bfloat16),
        preferred_element_type=jnp.float32,
    )
    keys = jnp.where(tiles > 0.5, ranks, -1.0)
    counts = tiles.sum(axis=1).astype(jnp.int32)
    counts = (counts + ALIGN - 1) // ALIGN * ALIGN
    order = jnp.arange(n_tiles + 1)
    offs = jnp.where(order[:n_tiles][None] < order[:, None], counts[None], 0).sum(axis=1)

    room = -(-(n_tiles * TILE + TILE) // ROWS) * ROWS
    wide = lat + BLOCK + 2 * PAD
    buf = pltpu.VMEM((2, lon + 2 * HALO, wide, feat // 2), jnp.float32)
    hidden = w_first.shape[1]
    return pl.pallas_call(
        kernel,
        out_shape=jax.ShapeDtypeStruct(state_in.shape, jnp.float32),
        in_specs=[anywhere] * 6 + [vmem, vmem, smem] + [anywhere] * 3,
        out_specs=anywhere,
        scratch_shapes=[
            buf,
            buf,
            pltpu.VMEM((room, feat), jnp.bfloat16),
            pltpu.VMEM((ROWS, hidden), jnp.bfloat16),
            pltpu.VMEM((ROWS, hidden), jnp.bfloat16),
            pltpu.VMEM(w_first.shape, jnp.bfloat16),
            pltpu.VMEM(w_hidden.shape, jnp.bfloat16),
            pltpu.VMEM(w_last.shape, jnp.bfloat16),
            pltpu.VMEM((2,) + north.shape, jnp.bfloat16),
            pltpu.SemaphoreType.DMA((10,)),
            pltpu.SemaphoreType.DMA((3,)),
            pltpu.SemaphoreType.DMA((8,)),
        ],
        compiler_params=pltpu.CompilerParams(vmem_limit_bytes=50 * 1024 * 1024),
    )(
        state_in, north, south, side, corner_n, corner_s, diffusion[None], keys, offs,
        w_first, w_hidden, w_last,
    )


def solution(mesh):
    return jax.shard_map(
        functools.partial(local, mesh.shape["lon"]),
        mesh=mesh,
        in_specs=(
            P(("ens", "lon"), "lat", None),
            P(),
            P(("ens", "lon"), "lat", None),
            P("ens", None, "lat"),
            P(),
            P(),
            P(),
        ),
        out_specs=P(("ens", "lon"), "lat", None),
        check_vma=False,
    )
```

```python
import functools

import jax
import jax.numpy as jnp
from jax import lax
from jax.experimental import pallas as pl
from jax.experimental.pallas import tpu as pltpu
from jax.sharding import PartitionSpec as P

HALO = 4
BLOCK = 8
PAD = 8
ALIGN = 16
TILE = 256
ROWS = 512
LANES = 128


def silu(u):
    half = 0.5 * u
    return half + half * jnp.tanh(half)


def kernel(
    state, north, south, side, corner_n, corner_s, diffusion, keys, offs,
    w_first, w_hidden, w_last, out,
    a_buf, b_buf, packed, hid_a, hid_b, w1, wh, w3, rows_in, in_sem, w_sem, out_sem,
):
    lon, lat, feat = state.shape
    lanes = feat // 2
    me = lax.axis_index("lat")
    own = pl.multiple_of(PAD + BLOCK * me, BLOCK)
    beside = pl.multiple_of(jnp.where(me == 0, PAD + lat, PAD), BLOCK)
    top, low = HALO, HALO + lon

    copies = []
    for half in range(2):
        cut = pl.ds(half * lanes, lanes)
        for source, row, rows, place, width in (
            (side, top, lon, beside, BLOCK),
            (corner_n, 0, HALO, beside, BLOCK),
            (corner_s, low, HALO, beside, BLOCK),
            (state, top, lon, own, lat),
        ):
            copies.append(
                pltpu.make_async_copy(
                    source.at[:, :, cut],
                    a_buf.at[half, pl.ds(row, rows), pl.ds(place, width), :],
                    in_sem.at[len(copies)],
                )
            )
    for source, which in ((north, 0), (south, 1)):
        copies.append(pltpu.make_async_copy(source, rows_in.at[which], in_sem.at[len(copies)]))
    weights = [
        pltpu.make_async_copy(w_first, w1, w_sem.at[0]),
        pltpu.make_async_copy(w_hidden, wh, w_sem.at[1]),
        pltpu.make_async_copy(w_last, w3, w_sem.at[2]),
    ]
    for copy in copies:
        copy.start()
    for copy in weights:
        copy.start()
    wide = a_buf.shape[2] - 2 * PAD

    def clear(row, carry):
        for buf in (a_buf, b_buf):
            for half in range(2):
                buf[half, row, 0:PAD, :] = jnp.zeros((PAD, lanes), jnp.float32)
                buf[half, row, PAD + wide :, :] = jnp.zeros((PAD, lanes), jnp.float32)
        return carry

    lax.fori_loop(0, a_buf.shape[1], clear, 0)
    for copy in copies:
        copy.wait()
    for which, row in ((0, 0), (1, low)):
        for half in range(2):
            cells = rows_in[which, :, :, half * lanes : (half + 1) * lanes].astype(jnp.float32)
            a_buf[half, row : row + HALO, pl.ds(own, lat), :] = cells

    def sweep(src, dst, first, last):
        unroll = next(size for size in (4, 7, 2, 1) if (last - first) % size == 0)

        def row_step(row, carry):
            for half in range(2):
                amount = diffusion[0:1, half * lanes : (half + 1) * lanes]
                keep = 1.0 - 4.0 * amount
                here = src[half, row, PAD : PAD + wide, :]
                around = (
                    src[half, row - 1, PAD : PAD + wide, :]
                    + src[half, row + 1, PAD : PAD + wide, :]
                ) + (
                    src[half, row, PAD - 1 : PAD + wide - 1, :]
                    + src[half, row, PAD + 1 : PAD + wide + 1, :]
                )
                dst[half, row, PAD : PAD + wide, :] = keep * here + amount * around
            return carry

        lax.fori_loop(first, last, row_step, 0, unroll=unroll)

    sweep(a_buf, b_buf, 1, low + HALO - 1)
    sweep(b_buf, a_buf, 2, low + HALO - 2)

    per_tile = TILE // lat
    pieces = [
        [(HALO - 1, 1, beside, BLOCK), (low, 1, beside, BLOCK)],
        [(top, lon // 2, beside, BLOCK)],
        [(top + lon // 2, lon // 2, beside, BLOCK)],
        [(HALO - 2, 2, own, lat), (low, 2, own, lat)],
    ]
    n_side = len(pieces)
    n_main = lon // per_tile

    def select(tile, width):
        spot = lax.broadcasted_iota(jnp.int32, (TILE, width), 0).astype(jnp.float32)
        return jnp.where(spot == keys[pl.ds(tile, 1), 0:width], 1.0, 0.0).astype(jnp.bfloat16)

    def gather(tile, slices):
        halves = [
            jnp.concatenate(
                [
                    a_buf[half, pl.ds(row, rows), pl.ds(place, width), :].reshape(rows * width, lanes)
                    for row, rows, place, width in slices
                ],
                axis=0,
            ).astype(jnp.bfloat16)
            for half in range(2)
        ]
        values = jnp.concatenate(halves, axis=1)
        picked = jnp.dot(select(tile, values.shape[0]), values, preferred_element_type=jnp.float32)
        start = pl.multiple_of(offs[tile, 0], ALIGN)
        packed[pl.ds(start, TILE), :] = picked.astype(jnp.bfloat16)

    def scatter(tile, slices):
        start = pl.multiple_of(offs[tile, 0], ALIGN)
        change = packed[pl.ds(start, TILE), :]
        count = sum(rows * width for _, rows, _, width in slices)
        spread = lax.dot_general(
            select(tile, count), change, (((0,), (0,)), ((), ())), preferred_element_type=jnp.float32
        )
        for half in range(2):
            done = 0
            for row, rows, place, width in slices:
                part = spread[done : done + rows * width, half * lanes : (half + 1) * lanes]
                done += rows * width
                where = (half, pl.ds(row, rows), pl.ds(place, width), slice(None))
                a_buf[where] = a_buf[where] + part.reshape(rows, width, lanes)

    for tile, slices in enumerate(pieces):
        gather(tile, slices)

    def main_gather(step, carry):
        gather(n_side + step, [(top + per_tile * step, per_tile, own, lat)])
        return carry

    lax.fori_loop(0, n_main, main_gather, 0, unroll=4)
    for copy in weights:
        copy.wait()

    hidden = w1.shape[1]

    def layer(x, weight, dst):
        for column in range(0, hidden, TILE):
            u = jnp.dot(x, weight[:, column : column + TILE], preferred_element_type=jnp.float32)
            dst[:, column : column + TILE] = silu(u).astype(jnp.bfloat16)

    def network(step, carry):
        rows = pl.ds(pl.multiple_of(step * ROWS, ROWS), ROWS)
        layer(packed[rows, :], w1, hid_a)
        now, other = hid_a, hid_b
        for middle in range(wh.shape[0]):
            layer(now[...], wh.at[middle], other)
            now, other = other, now
        packed[rows, :] = jnp.dot(now[...], w3[...], preferred_element_type=jnp.float32).astype(
            jnp.bfloat16
        )
        return carry

    total = offs[n_side + n_main, 0]
    lax.fori_loop(0, (total + ROWS - 1) // ROWS, network, 0)

    for tile, slices in enumerate(pieces):
        scatter(tile, slices)

    def main_scatter(step, carry):
        scatter(n_side + step, [(top + per_tile * step, per_tile, own, lat)])
        return carry

    lax.fori_loop(0, n_main, main_scatter, 0, unroll=4)

    sweep(a_buf, b_buf, 2, low + HALO - 2)
    parts = 4
    outs = []
    for part in range(parts):
        begin = part * lon // parts
        size = (part + 1) * lon // parts - begin
        sweep(b_buf, a_buf, top + begin, top + begin + size)
        for half in range(2):
            copy = pltpu.make_async_copy(
                a_buf.at[half, pl.ds(top + begin, size), pl.ds(own, lat), :],
                out.at[pl.ds(begin, size), :, pl.ds(half * lanes, lanes)],
                out_sem.at[len(outs)],
            )
            copy.start()
            outs.append(copy)
    for copy in outs:
        copy.wait()


def exchange(
    n_lon, state, listed, counts,
    north, south, side, corner_n, corner_s, keys, offs,
    tiles, mine, strip, above, below, other, above_x, below_x, edges, lines, edge_sem, send_sem, recv_sem,
):
    lon, lat, _ = state.shape
    place, me = lax.axis_index("lon"), lax.axis_index("lat")
    east, west, across = lax.rem(place + 1, n_lon), lax.rem(place + n_lon - 1, n_lon), 1 - me
    others = [(west, me), (east, me), (place, across), (west, across), (east, across)]

    def device(spot):
        return {"lon": spot[0], "lat": spot[1]}

    loads = [
        pltpu.make_async_copy(state.at[pl.ds(row, HALO)], edges.at[which], edge_sem.at[which])
        for which, row in ((0, 0), (1, lon - HALO))
    ]
    for load in loads:
        load.start()
    barrier = pltpu.get_barrier_semaphore()
    for spot in others:
        pl.semaphore_signal(
            barrier, inc=1, device_id=device(spot), device_id_type=pl.DeviceIdType.MESH
        )
    pl.semaphore_wait(barrier, len(others))

    sent = []

    def send(source, target, spot):
        copy = pltpu.make_async_remote_copy(
            src_ref=source,
            dst_ref=target,
            send_sem=send_sem.at[len(sent)],
            recv_sem=recv_sem.at[len(sent)],
            device_id=device(spot),
            device_id_type=pl.DeviceIdType.MESH,
        )
        copy.start()
        sent.append(copy)

    for which, target, spot in ((0, south, others[0]), (1, north, others[1])):
        loads[which].wait()
        lines[which] = edges[which].astype(jnp.bfloat16)
        send(lines.at[which], target, spot)
    cut = pl.ds(pl.multiple_of(jnp.where(me == 0, lat - BLOCK, 0), BLOCK), BLOCK)
    send(state.at[pl.ds(0, HALO), cut], corner_s, others[3])
    send(state.at[pl.ds(lon - HALO, HALO), cut], corner_n, others[4])
    send(state.at[:, cut], side, others[2])

    numbers = listed[...]
    length = numbers.shape[1]
    active = lax.broadcasted_iota(jnp.int32, (1, length), 1) < counts[place]
    numbers = jnp.where(active, numbers, -1)
    rows = lax.shift_right_arithmetic(numbers, jnp.int32(lat.bit_length() - 1))
    spots = numbers & (lat - 1)

    def hot(number, size):
        same = lax.broadcasted_iota(jnp.int32, (size, length), 0) == number
        return jnp.where(same, 1.0, 0.0).astype(jnp.bfloat16)

    def marks(tile, position, size):
        return lax.dot_general(
            hot(tile, size), hot(position, TILE), (((1,), (1,)), ((), ())),
            preferred_element_type=jnp.float32,
        )

    n_main = lon * lat // TILE
    mine[...] = marks(
        lax.shift_right_arithmetic(numbers, jnp.int32(TILE.bit_length() - 1)), numbers & (TILE - 1), n_main
    )
    height = TILE // BLOCK
    reached = jnp.where(me == 0, lat - 2, 0)
    close = (spots >= reached) & (spots < reached + 2)
    strip_tile = jnp.where(
        close, lax.shift_right_arithmetic(rows, jnp.int32(height.bit_length() - 1)), -1
    )
    strip[...] = marks(strip_tile, (rows & (height - 1)) * BLOCK + (spots & (BLOCK - 1)), BLOCK)
    send(mine.at[pl.ds(0, BLOCK)], below, others[0])
    send(mine.at[pl.ds(n_main - BLOCK, BLOCK)], above, others[1])
    send(strip, below_x, others[3])
    send(strip, above_x, others[4])
    send(strip, other, others[2])
    for copy in sent:
        copy.wait()

    n_strip = lon // height
    lane = lax.broadcasted_iota(jnp.int32, (BLOCK, TILE), 1)
    from_n = pltpu.roll(above_x[...], BLOCK, 1)[n_strip - 1 : n_strip]
    from_s = pltpu.roll(below_x[...], BLOCK, 1)[0:1]
    lane = lane[0:1]
    tiles[0:1, :] = jnp.where(lane < BLOCK, from_n, jnp.where(lane < 2 * BLOCK, from_s, 0.0))
    tiles[1 : 1 + n_strip, :] = other[0:n_strip, :]
    near = 2 * lat
    tiles[1 + n_strip : 2 + n_strip, 0:near] = above[BLOCK - 1 : BLOCK, TILE - near :]
    tiles[1 + n_strip : 2 + n_strip, near:] = below[0:1, 0:near]
    filled = 2 + n_strip + n_main
    tiles[2 + n_strip : filled, :] = mine[...]
    size = tiles.shape[0]
    if filled < size:
        tiles[filled:, :] = jnp.zeros((size - filled, TILE), jnp.float32)
    marked = tiles[...]
    before = jnp.where(
        lax.broadcasted_iota(jnp.int32, (TILE, TILE), 0) < lax.broadcasted_iota(jnp.int32, (TILE, TILE), 1),
        1.0,
        0.0,
    ).astype(jnp.bfloat16)
    ranks = jnp.dot(marked.astype(jnp.bfloat16), before, preferred_element_type=jnp.float32)
    keys[...] = jnp.where(marked > 0.5, ranks, -1.0)
    counts = jnp.sum(marked, axis=1, keepdims=True)
    counts = jnp.floor((counts + (ALIGN - 1)) * (1.0 / ALIGN)) * ALIGN
    earlier = jnp.where(
        lax.broadcasted_iota(jnp.int32, (size, size), 1) < lax.broadcasted_iota(jnp.int32, (size, size), 0),
        1.0,
        0.0,
    ).astype(jnp.bfloat16)
    offs[...] = jnp.dot(
        earlier,
        jnp.broadcast_to(counts, (size, offs.shape[1])).astype(jnp.bfloat16),
        preferred_element_type=jnp.float32,
    ).astype(jnp.int32)


def local(n_lon, state_in, diffusion, conv_index, conv_count, w_first, w_hidden, w_last):
    lon, lat, feat = state_in.shape

    listed = conv_index.reshape(1, -1)
    anywhere = pl.BlockSpec(memory_space=pltpu.HBM)
    vmem = pl.BlockSpec(memory_space=pltpu.VMEM)
    smem = pl.BlockSpec(memory_space=pltpu.SMEM)
    shape = jax.ShapeDtypeStruct
    lines = shape((HALO, lat, feat), jnp.bfloat16)
    block = shape((HALO, BLOCK, feat), jnp.float32)
    n_tiles = 2 + lon * BLOCK // TILE + lon * lat // TILE
    padded = -(-(n_tiles + 1) // 8) * 8
    few = pltpu.VMEM((BLOCK, TILE), jnp.float32)
    north, south, side, corner_n, corner_s, keys, offs = pl.pallas_call(
        functools.partial(exchange, n_lon),
        out_shape=(lines, lines, shape((lon, BLOCK, feat), jnp.float32), block, block)
        + (shape((padded, TILE), jnp.float32), shape((padded, LANES), jnp.int32)),
        in_specs=[anywhere, vmem, smem],
        out_specs=(anywhere,) * 5 + (vmem, vmem),
        scratch_shapes=[
            pltpu.VMEM((padded, TILE), jnp.float32),
            pltpu.VMEM((lon * lat // TILE, TILE), jnp.float32),
            few, few, few, few, few, few,
            pltpu.VMEM((2, HALO, lat, feat), jnp.float32),
            pltpu.VMEM((2, HALO, lat, feat), jnp.bfloat16),
            pltpu.SemaphoreType.DMA((2,)),
            pltpu.SemaphoreType.DMA((10,)),
            pltpu.SemaphoreType.DMA((10,)),
        ],
        compiler_params=pltpu.CompilerParams(
            collective_id=0, has_side_effects=True, vmem_limit_bytes=60 * 1024 * 1024
        ),
    )(state_in, listed, conv_count[0, :, 0])
    room = -(-(n_tiles * TILE + TILE) // ROWS) * ROWS
    wide = lat + BLOCK + 2 * PAD
    buf = pltpu.VMEM((2, lon + 2 * HALO, wide, feat // 2), jnp.float32)
    hidden = w_first.shape[1]
    return pl.pallas_call(
        kernel,
        out_shape=jax.ShapeDtypeStruct(state_in.shape, jnp.float32),
        in_specs=[anywhere] * 6 + [vmem, vmem, smem] + [anywhere] * 3,
        out_specs=anywhere,
        scratch_shapes=[
            buf,
            buf,
            pltpu.VMEM((room, feat), jnp.bfloat16),
            pltpu.VMEM((ROWS, hidden), jnp.bfloat16),
            pltpu.VMEM((ROWS, hidden), jnp.bfloat16),
            pltpu.VMEM(w_first.shape, jnp.bfloat16),
            pltpu.VMEM(w_hidden.shape, jnp.bfloat16),
            pltpu.VMEM(w_last.shape, jnp.bfloat16),
            pltpu.VMEM((2,) + north.shape, jnp.bfloat16),
            pltpu.SemaphoreType.DMA((10,)),
            pltpu.SemaphoreType.DMA((3,)),
            pltpu.SemaphoreType.DMA((8,)),
        ],
        compiler_params=pltpu.CompilerParams(vmem_limit_bytes=60 * 1024 * 1024),
    )(
        state_in, north, south, side, corner_n, corner_s, diffusion[None], keys, offs,
        w_first, w_hidden, w_last,
    )


def solution(mesh):
    return jax.shard_map(
        functools.partial(local, mesh.shape["lon"]),
        mesh=mesh,
        in_specs=(
            P(("ens", "lon"), "lat", None),
            P(),
            P(("ens", "lon"), "lat", None),
            P("ens", None, "lat"),
            P(),
            P(),
            P(),
        ),
        out_specs=P(("ens", "lon"), "lat", None),
        check_vma=False,
    )
```

```python
import functools

import jax
import jax.numpy as jnp
from jax import lax
from jax.experimental import pallas as pl
from jax.experimental.pallas import tpu as pltpu
from jax.sharding import PartitionSpec as P

HALO = 4
BLOCK = 8
PAD = 8
ALIGN = 16
TILE = 256
ROWS = 512
LANES = 128


def silu(u):
    half = 0.5 * u
    return half + half * jnp.tanh(half)


def kernel(
    state, north, south, side, corner_n, corner_s, diffusion, keys, offs,
    w_first, w_hidden, w_last, out,
    a_buf, b_buf, packed, hid_a, hid_b, w1, wh, w3, rows_in, in_sem, w_sem, out_sem,
):
    lon, lat, feat = state.shape
    lanes = feat // 2
    me = lax.axis_index("lat")
    own = pl.multiple_of(PAD + BLOCK * me, BLOCK)
    beside = pl.multiple_of(jnp.where(me == 0, PAD + lat, PAD), BLOCK)
    top, low = HALO, HALO + lon

    copies = []
    for half in range(2):
        cut = pl.ds(half * lanes, lanes)
        for source, row, rows, place, width in (
            (side, top, lon, beside, BLOCK),
            (corner_n, 0, HALO, beside, BLOCK),
            (corner_s, low, HALO, beside, BLOCK),
        ):
            copies.append(
                pltpu.make_async_copy(
                    source.at[:, :, cut],
                    a_buf.at[half, pl.ds(row, rows), pl.ds(place, width), :],
                    in_sem.at[len(copies)],
                )
            )
    for source, which in ((north, 0), (south, 1)):
        copies.append(pltpu.make_async_copy(source, rows_in.at[which], in_sem.at[len(copies)]))
    weights = [
        pltpu.make_async_copy(w_first, w1, w_sem.at[0]),
        pltpu.make_async_copy(w_hidden, wh, w_sem.at[1]),
        pltpu.make_async_copy(w_last, w3, w_sem.at[2]),
    ]
    parts = 4
    cuts = [part * lon // parts for part in range(parts + 1)]
    chunks = []
    for part in range(parts):
        rows = pl.ds(cuts[part], cuts[part + 1] - cuts[part])
        chunks.append(
            [
                pltpu.make_async_copy(
                    state.at[rows, :, pl.ds(half * lanes, lanes)],
                    a_buf.at[
                        half, pl.ds(top + cuts[part], cuts[part + 1] - cuts[part]), pl.ds(own, lat), :
                    ],
                    in_sem.at[len(copies) + 2 * part + half],
                )
                for half in range(2)
            ]
        )
    for copy in copies + sum(chunks, []):
        copy.start()
    wide = a_buf.shape[2] - 2 * PAD

    def clear(row, carry):
        for buf in (a_buf, b_buf):
            for half in range(2):
                buf[half, row, 0:PAD, :] = jnp.zeros((PAD, lanes), jnp.float32)
                buf[half, row, PAD + wide :, :] = jnp.zeros((PAD, lanes), jnp.float32)
        return carry

    lax.fori_loop(0, a_buf.shape[1], clear, 0)
    for copy in copies:
        copy.wait()
    for which, row in ((0, 0), (1, low)):
        for half in range(2):
            cells = rows_in[which, :, :, half * lanes : (half + 1) * lanes].astype(jnp.float32)
            a_buf[half, row : row + HALO, pl.ds(own, lat), :] = cells

    def sweep(src, dst, first, last):
        unroll = next(size for size in (4, 7, 2, 1) if (last - first) % size == 0)

        def row_step(row, carry):
            for half in range(2):
                amount = diffusion[0:1, half * lanes : (half + 1) * lanes]
                keep = 1.0 - 4.0 * amount
                here = src[half, row, PAD : PAD + wide, :]
                around = (
                    src[half, row - 1, PAD : PAD + wide, :]
                    + src[half, row + 1, PAD : PAD + wide, :]
                ) + (
                    src[half, row, PAD - 1 : PAD + wide - 1, :]
                    + src[half, row, PAD + 1 : PAD + wide + 1, :]
                )
                dst[half, row, PAD : PAD + wide, :] = keep * here + amount * around
            return carry

        lax.fori_loop(first, last, row_step, 0, unroll=unroll)

    begin = 1
    for part in range(parts):
        for copy in chunks[part]:
            copy.wait()
        if part == parts - 1:
            for copy in weights:
                copy.start()
        end = low + HALO - 1 if part == parts - 1 else top + cuts[part + 1] - 1
        sweep(a_buf, b_buf, begin, end)
        begin = end
    sweep(b_buf, a_buf, 2, low + HALO - 2)

    per_tile = TILE // lat
    pieces = [
        [(HALO - 1, 1, beside, BLOCK), (low, 1, beside, BLOCK)],
        [(top, lon // 2, beside, BLOCK)],
        [(top + lon // 2, lon // 2, beside, BLOCK)],
        [(HALO - 2, 2, own, lat), (low, 2, own, lat)],
    ]
    n_side = len(pieces)
    n_main = lon // per_tile

    def select(tile, width):
        spot = lax.broadcasted_iota(jnp.int32, (TILE, width), 0).astype(jnp.float32)
        return jnp.where(spot == keys[pl.ds(tile, 1), 0:width], 1.0, 0.0).astype(jnp.bfloat16)

    def gather(tile, slices):
        halves = [
            jnp.concatenate(
                [
                    a_buf[half, pl.ds(row, rows), pl.ds(place, width), :].reshape(rows * width, lanes)
                    for row, rows, place, width in slices
                ],
                axis=0,
            ).astype(jnp.bfloat16)
            for half in range(2)
        ]
        values = jnp.concatenate(halves, axis=1)
        picked = jnp.dot(select(tile, values.shape[0]), values, preferred_element_type=jnp.float32)
        start = pl.multiple_of(offs[tile, 0], ALIGN)
        packed[pl.ds(start, TILE), :] = picked.astype(jnp.bfloat16)

    def scatter(tile, slices):
        start = pl.multiple_of(offs[tile, 0], ALIGN)
        change = packed[pl.ds(start, TILE), :]
        count = sum(rows * width for _, rows, _, width in slices)
        spread = lax.dot_general(
            select(tile, count), change, (((0,), (0,)), ((), ())), preferred_element_type=jnp.float32
        )
        for half in range(2):
            done = 0
            for row, rows, place, width in slices:
                part = spread[done : done + rows * width, half * lanes : (half + 1) * lanes]
                done += rows * width
                where = (half, pl.ds(row, rows), pl.ds(place, width), slice(None))
                a_buf[where] = a_buf[where] + part.reshape(rows, width, lanes)

    for tile, slices in enumerate(pieces):
        gather(tile, slices)

    def main_gather(step, carry):
        gather(n_side + step, [(top + per_tile * step, per_tile, own, lat)])
        return carry

    lax.fori_loop(0, n_main, main_gather, 0, unroll=4)
    for copy in weights:
        copy.wait()

    hidden = w1.shape[1]

    def layer(x, weight, dst):
        for column in range(0, hidden, TILE):
            u = jnp.dot(x, weight[:, column : column + TILE], preferred_element_type=jnp.float32)
            dst[:, column : column + TILE] = silu(u).astype(jnp.bfloat16)

    def network(step, carry):
        rows = pl.ds(pl.multiple_of(step * ROWS, ROWS), ROWS)
        layer(packed[rows, :], w1, hid_a)
        now, other = hid_a, hid_b
        for middle in range(wh.shape[0]):
            layer(now[...], wh.at[middle], other)
            now, other = other, now
        packed[rows, :] = jnp.dot(now[...], w3[...], preferred_element_type=jnp.float32).astype(
            jnp.bfloat16
        )
        return carry

    total = offs[n_side + n_main, 0]
    lax.fori_loop(0, (total + ROWS - 1) // ROWS, network, 0)

    for tile, slices in enumerate(pieces):
        scatter(tile, slices)

    def main_scatter(step, carry):
        scatter(n_side + step, [(top + per_tile * step, per_tile, own, lat)])
        return carry

    lax.fori_loop(0, n_main, main_scatter, 0, unroll=4)

    sweep(a_buf, b_buf, 2, low + HALO - 2)
    outs = []
    for part in range(parts):
        begin = part * lon // parts
        size = (part + 1) * lon // parts - begin
        sweep(b_buf, a_buf, top + begin, top + begin + size)
        for half in range(2):
            copy = pltpu.make_async_copy(
                a_buf.at[half, pl.ds(top + begin, size), pl.ds(own, lat), :],
                out.at[pl.ds(begin, size), :, pl.ds(half * lanes, lanes)],
                out_sem.at[len(outs)],
            )
            copy.start()
            outs.append(copy)
    for copy in outs:
        copy.wait()


def exchange(
    n_lon, state, listed, counts,
    north, south, side, corner_n, corner_s, keys, offs,
    tiles, mine, strip, above, below, other, above_x, below_x, edges, lines, edge_sem, send_sem, recv_sem,
):
    lon, lat, _ = state.shape
    place, me = lax.axis_index("lon"), lax.axis_index("lat")
    east, west, across = lax.rem(place + 1, n_lon), lax.rem(place + n_lon - 1, n_lon), 1 - me
    others = [(west, me), (east, me), (place, across), (west, across), (east, across)]

    def device(spot):
        return {"lon": spot[0], "lat": spot[1]}

    loads = [
        pltpu.make_async_copy(state.at[pl.ds(row, HALO)], edges.at[which], edge_sem.at[which])
        for which, row in ((0, 0), (1, lon - HALO))
    ]
    for load in loads:
        load.start()
    barrier = pltpu.get_barrier_semaphore()
    for spot in others:
        pl.semaphore_signal(
            barrier, inc=1, device_id=device(spot), device_id_type=pl.DeviceIdType.MESH
        )
    pl.semaphore_wait(barrier, len(others))

    sent = []

    def send(source, target, spot):
        copy = pltpu.make_async_remote_copy(
            src_ref=source,
            dst_ref=target,
            send_sem=send_sem.at[len(sent)],
            recv_sem=recv_sem.at[len(sent)],
            device_id=device(spot),
            device_id_type=pl.DeviceIdType.MESH,
        )
        copy.start()
        sent.append(copy)

    for which, target, spot in ((0, south, others[0]), (1, north, others[1])):
        loads[which].wait()
        lines[which] = edges[which].astype(jnp.bfloat16)
        send(lines.at[which], target, spot)
    cut = pl.ds(pl.multiple_of(jnp.where(me == 0, lat - BLOCK, 0), BLOCK), BLOCK)
    send(state.at[pl.ds(0, HALO), cut], corner_s, others[3])
    send(state.at[pl.ds(lon - HALO, HALO), cut], corner_n, others[4])
    send(state.at[:, cut], side, others[2])

    numbers = listed[...]
    length = numbers.shape[1]
    active = lax.broadcasted_iota(jnp.int32, (1, length), 1) < counts[place]
    numbers = jnp.where(active, numbers, -1)
    rows = lax.shift_right_arithmetic(numbers, jnp.int32(lat.bit_length() - 1))
    spots = numbers & (lat - 1)

    def hot(number, size):
        same = lax.broadcasted_iota(jnp.int32, (size, length), 0) == number
        return jnp.where(same, 1.0, 0.0).astype(jnp.bfloat16)

    def marks(tile, position, size):
        return lax.dot_general(
            hot(tile, size), hot(position, TILE), (((1,), (1,)), ((), ())),
            preferred_element_type=jnp.float32,
        )

    n_main = lon * lat // TILE
    mine[...] = marks(
        lax.shift_right_arithmetic(numbers, jnp.int32(TILE.bit_length() - 1)), numbers & (TILE - 1), n_main
    )
    height = TILE // BLOCK
    reached = jnp.where(me == 0, lat - 2, 0)
    close = (spots >= reached) & (spots < reached + 2)
    strip_tile = jnp.where(
        close, lax.shift_right_arithmetic(rows, jnp.int32(height.bit_length() - 1)), -1
    )
    strip[...] = marks(strip_tile, (rows & (height - 1)) * BLOCK + (spots & (BLOCK - 1)), BLOCK)
    send(mine.at[pl.ds(0, BLOCK)], below, others[0])
    send(mine.at[pl.ds(n_main - BLOCK, BLOCK)], above, others[1])
    send(strip, below_x, others[3])
    send(strip, above_x, others[4])
    send(strip, other, others[2])
    for copy in sent:
        copy.wait()

    n_strip = lon // height
    lane = lax.broadcasted_iota(jnp.int32, (BLOCK, TILE), 1)
    from_n = pltpu.roll(above_x[...], BLOCK, 1)[n_strip - 1 : n_strip]
    from_s = pltpu.roll(below_x[...], BLOCK, 1)[0:1]
    lane = lane[0:1]
    tiles[0:1, :] = jnp.where(lane < BLOCK, from_n, jnp.where(lane < 2 * BLOCK, from_s, 0.0))
    tiles[1 : 1 + n_strip, :] = other[0:n_strip, :]
    near = 2 * lat
    tiles[1 + n_strip : 2 + n_strip, 0:near] = above[BLOCK - 1 : BLOCK, TILE - near :]
    tiles[1 + n_strip : 2 + n_strip, near:] = below[0:1, 0:near]
    filled = 2 + n_strip + n_main
    tiles[2 + n_strip : filled, :] = mine[...]
    size = tiles.shape[0]
    if filled < size:
        tiles[filled:, :] = jnp.zeros((size - filled, TILE), jnp.float32)
    marked = tiles[...]
    before = jnp.where(
        lax.broadcasted_iota(jnp.int32, (TILE, TILE), 0) < lax.broadcasted_iota(jnp.int32, (TILE, TILE), 1),
        1.0,
        0.0,
    ).astype(jnp.bfloat16)
    ranks = jnp.dot(marked.astype(jnp.bfloat16), before, preferred_element_type=jnp.float32)
    keys[...] = jnp.where(marked > 0.5, ranks, -1.0)
    counts = jnp.sum(marked, axis=1, keepdims=True)
    counts = jnp.floor((counts + (ALIGN - 1)) * (1.0 / ALIGN)) * ALIGN
    earlier = jnp.where(
        lax.broadcasted_iota(jnp.int32, (size, size), 1) < lax.broadcasted_iota(jnp.int32, (size, size), 0),
        1.0,
        0.0,
    ).astype(jnp.bfloat16)
    offs[...] = jnp.dot(
        earlier,
        jnp.broadcast_to(counts, (size, offs.shape[1])).astype(jnp.bfloat16),
        preferred_element_type=jnp.float32,
    ).astype(jnp.int32)


def local(n_lon, state_in, diffusion, conv_index, conv_count, w_first, w_hidden, w_last):
    lon, lat, feat = state_in.shape

    listed = conv_index.reshape(1, -1)
    anywhere = pl.BlockSpec(memory_space=pltpu.HBM)
    vmem = pl.BlockSpec(memory_space=pltpu.VMEM)
    smem = pl.BlockSpec(memory_space=pltpu.SMEM)
    shape = jax.ShapeDtypeStruct
    lines = shape((HALO, lat, feat), jnp.bfloat16)
    block = shape((HALO, BLOCK, feat), jnp.float32)
    n_tiles = 2 + lon * BLOCK // TILE + lon * lat // TILE
    padded = -(-(n_tiles + 1) // 8) * 8
    few = pltpu.VMEM((BLOCK, TILE), jnp.float32)
    north, south, side, corner_n, corner_s, keys, offs = pl.pallas_call(
        functools.partial(exchange, n_lon),
        out_shape=(lines, lines, shape((lon, BLOCK, feat), jnp.float32), block, block)
        + (shape((padded, TILE), jnp.float32), shape((padded, LANES), jnp.int32)),
        in_specs=[anywhere, vmem, smem],
        out_specs=(anywhere,) * 5 + (vmem, vmem),
        scratch_shapes=[
            pltpu.VMEM((padded, TILE), jnp.float32),
            pltpu.VMEM((lon * lat // TILE, TILE), jnp.float32),
            few, few, few, few, few, few,
            pltpu.VMEM((2, HALO, lat, feat), jnp.float32),
            pltpu.VMEM((2, HALO, lat, feat), jnp.bfloat16),
            pltpu.SemaphoreType.DMA((2,)),
            pltpu.SemaphoreType.DMA((10,)),
            pltpu.SemaphoreType.DMA((10,)),
        ],
        compiler_params=pltpu.CompilerParams(
            collective_id=0, has_side_effects=True, vmem_limit_bytes=60 * 1024 * 1024
        ),
    )(state_in, listed, conv_count[0, :, 0])
    room = -(-(n_tiles * TILE + TILE) // ROWS) * ROWS
    wide = lat + BLOCK + 2 * PAD
    buf = pltpu.VMEM((2, lon + 2 * HALO, wide, feat // 2), jnp.float32)
    hidden = w_first.shape[1]
    return pl.pallas_call(
        kernel,
        out_shape=jax.ShapeDtypeStruct(state_in.shape, jnp.float32),
        in_specs=[anywhere] * 6 + [vmem, vmem, smem] + [anywhere] * 3,
        out_specs=anywhere,
        scratch_shapes=[
            buf,
            buf,
            pltpu.VMEM((room, feat), jnp.bfloat16),
            pltpu.VMEM((ROWS, hidden), jnp.bfloat16),
            pltpu.VMEM((ROWS, hidden), jnp.bfloat16),
            pltpu.VMEM(w_first.shape, jnp.bfloat16),
            pltpu.VMEM(w_hidden.shape, jnp.bfloat16),
            pltpu.VMEM(w_last.shape, jnp.bfloat16),
            pltpu.VMEM((2,) + north.shape, jnp.bfloat16),
            pltpu.SemaphoreType.DMA((16,)),
            pltpu.SemaphoreType.DMA((3,)),
            pltpu.SemaphoreType.DMA((8,)),
        ],
        compiler_params=pltpu.CompilerParams(vmem_limit_bytes=60 * 1024 * 1024),
    )(
        state_in, north, south, side, corner_n, corner_s, diffusion[None], keys, offs,
        w_first, w_hidden, w_last,
    )


def solution(mesh):
    return jax.shard_map(
        functools.partial(local, mesh.shape["lon"]),
        mesh=mesh,
        in_specs=(
            P(("ens", "lon"), "lat", None),
            P(),
            P(("ens", "lon"), "lat", None),
            P("ens", None, "lat"),
            P(),
            P(),
            P(),
        ),
        out_specs=P(("ens", "lon"), "lat", None),
        check_vma=False,
    )
```

```python
import functools

import jax
import jax.numpy as jnp
from jax import lax
from jax.experimental import pallas as pl
from jax.experimental.pallas import tpu as pltpu
from jax.sharding import PartitionSpec as P

HALO = 4
BLOCK = 8
PAD = 8
ALIGN = 16
TILE = 256
ROWS = 512
LANES = 128


def silu(u):
    half = 0.5 * u
    return half + half * jnp.tanh(half)


def kernel(
    state, north, south, side, corner_n, corner_s, diffusion, keys, offs,
    w_first, w_hidden, w_last, out,
    a_buf, b_buf, packed, hid_a, hid_b, w1, wh, w3, rows_in, nooks_in, in_sem, w_sem, out_sem,
):
    lon, lat, feat = state.shape
    lanes = feat // 2
    me = lax.axis_index("lat")
    own = pl.multiple_of(PAD + BLOCK * me, BLOCK)
    beside = pl.multiple_of(jnp.where(me == 0, PAD + lat, PAD), BLOCK)
    top, low = HALO, HALO + lon

    copies = []
    for half in range(2):
        cut = pl.ds(half * lanes, lanes)
        for source, row, rows, place, width in (
            (side, top, lon, beside, BLOCK),
        ):
            copies.append(
                pltpu.make_async_copy(
                    source.at[:, :, cut],
                    a_buf.at[half, pl.ds(row, rows), pl.ds(place, width), :],
                    in_sem.at[len(copies)],
                )
            )
    for source, which in ((north, 0), (south, 1)):
        copies.append(pltpu.make_async_copy(source, rows_in.at[which], in_sem.at[len(copies)]))
    for source, which in ((corner_n, 0), (corner_s, 1)):
        copies.append(pltpu.make_async_copy(source, nooks_in.at[which], in_sem.at[len(copies)]))
    weights = [
        pltpu.make_async_copy(w_first, w1, w_sem.at[0]),
        pltpu.make_async_copy(w_hidden, wh, w_sem.at[1]),
        pltpu.make_async_copy(w_last, w3, w_sem.at[2]),
    ]
    parts = 4
    cuts = [part * lon // parts for part in range(parts + 1)]
    chunks = []
    for part in range(parts):
        rows = pl.ds(cuts[part], cuts[part + 1] - cuts[part])
        chunks.append(
            [
                pltpu.make_async_copy(
                    state.at[rows, :, pl.ds(half * lanes, lanes)],
                    a_buf.at[
                        half, pl.ds(top + cuts[part], cuts[part + 1] - cuts[part]), pl.ds(own, lat), :
                    ],
                    in_sem.at[len(copies) + 2 * part + half],
                )
                for half in range(2)
            ]
        )
    for copy in copies + sum(chunks, []):
        copy.start()
    wide = a_buf.shape[2] - 2 * PAD

    def clear(row, carry):
        for buf in (a_buf, b_buf):
            for half in range(2):
                buf[half, row, 0:PAD, :] = jnp.zeros((PAD, lanes), jnp.float32)
                buf[half, row, PAD + wide :, :] = jnp.zeros((PAD, lanes), jnp.float32)
        return carry

    lax.fori_loop(0, a_buf.shape[1], clear, 0)
    for copy in copies:
        copy.wait()
    for which, row in ((0, 0), (1, low)):
        for half in range(2):
            cells = rows_in[which, :, :, half * lanes : (half + 1) * lanes].astype(jnp.float32)
            a_buf[half, row : row + HALO, pl.ds(own, lat), :] = cells
            cells = nooks_in[which, :, half * lanes : (half + 1) * lanes].astype(jnp.float32)
            a_buf[half, row : row + HALO, pl.ds(beside, BLOCK), :] = cells.reshape(HALO, BLOCK, lanes)

    def sweep(src, dst, first, last):
        unroll = next(size for size in (4, 7, 2, 1) if (last - first) % size == 0)

        def row_step(row, carry):
            for half in range(2):
                amount = diffusion[0:1, half * lanes : (half + 1) * lanes]
                keep = 1.0 - 4.0 * amount
                here = src[half, row, PAD : PAD + wide, :]
                around = (
                    src[half, row - 1, PAD : PAD + wide, :]
                    + src[half, row + 1, PAD : PAD + wide, :]
                ) + (
                    src[half, row, PAD - 1 : PAD + wide - 1, :]
                    + src[half, row, PAD + 1 : PAD + wide + 1, :]
                )
                dst[half, row, PAD : PAD + wide, :] = keep * here + amount * around
            return carry

        lax.fori_loop(first, last, row_step, 0, unroll=unroll)

    begin = 1
    for part in range(parts):
        for copy in chunks[part]:
            copy.wait()
        if part == parts - 1:
            for copy in weights:
                copy.start()
        end = low + HALO - 1 if part == parts - 1 else top + cuts[part + 1] - 1
        sweep(a_buf, b_buf, begin, end)
        begin = end
    sweep(b_buf, a_buf, 2, low + HALO - 2)

    per_tile = TILE // lat
    pieces = [
        [(HALO - 1, 1, beside, BLOCK), (low, 1, beside, BLOCK)],
        [(top, lon // 2, beside, BLOCK)],
        [(top + lon // 2, lon // 2, beside, BLOCK)],
        [(HALO - 2, 2, own, lat), (low, 2, own, lat)],
    ]
    n_side = len(pieces)
    n_main = lon // per_tile

    def select(tile, width):
        spot = lax.broadcasted_iota(jnp.int32, (TILE, width), 0).astype(jnp.float32)
        return jnp.where(spot == keys[pl.ds(tile, 1), 0:width], 1.0, 0.0).astype(jnp.bfloat16)

    def gather(tile, slices):
        halves = [
            jnp.concatenate(
                [
                    a_buf[half, pl.ds(row, rows), pl.ds(place, width), :].reshape(rows * width, lanes)
                    for row, rows, place, width in slices
                ],
                axis=0,
            ).astype(jnp.bfloat16)
            for half in range(2)
        ]
        values = jnp.concatenate(halves, axis=1)
        picked = jnp.dot(select(tile, values.shape[0]), values, preferred_element_type=jnp.float32)
        start = pl.multiple_of(offs[tile, 0], ALIGN)
        packed[pl.ds(start, TILE), :] = picked.astype(jnp.bfloat16)

    def scatter(tile, slices):
        start = pl.multiple_of(offs[tile, 0], ALIGN)
        change = packed[pl.ds(start, TILE), :]
        count = sum(rows * width for _, rows, _, width in slices)
        spread = lax.dot_general(
            select(tile, count), change, (((0,), (0,)), ((), ())), preferred_element_type=jnp.float32
        )
        for half in range(2):
            done = 0
            for row, rows, place, width in slices:
                part = spread[done : done + rows * width, half * lanes : (half + 1) * lanes]
                done += rows * width
                where = (half, pl.ds(row, rows), pl.ds(place, width), slice(None))
                a_buf[where] = a_buf[where] + part.reshape(rows, width, lanes)

    for tile, slices in enumerate(pieces):
        gather(tile, slices)

    def main_gather(step, carry):
        gather(n_side + step, [(top + per_tile * step, per_tile, own, lat)])
        return carry

    lax.fori_loop(0, n_main, main_gather, 0, unroll=4)
    for copy in weights:
        copy.wait()

    hidden = w1.shape[1]

    def layer(x, weight, dst):
        for column in range(0, hidden, TILE):
            u = jnp.dot(x, weight[:, column : column + TILE], preferred_element_type=jnp.float32)
            dst[:, column : column + TILE] = silu(u).astype(jnp.bfloat16)

    def network(step, carry):
        rows = pl.ds(pl.multiple_of(step * ROWS, ROWS), ROWS)
        layer(packed[rows, :], w1, hid_a)
        now, other = hid_a, hid_b
        for middle in range(wh.shape[0]):
            layer(now[...], wh.at[middle], other)
            now, other = other, now
        packed[rows, :] = jnp.dot(now[...], w3[...], preferred_element_type=jnp.float32).astype(
            jnp.bfloat16
        )
        return carry

    total = offs[n_side + n_main, 0]
    lax.fori_loop(0, (total + ROWS - 1) // ROWS, network, 0)

    for tile, slices in enumerate(pieces):
        scatter(tile, slices)

    def main_scatter(step, carry):
        scatter(n_side + step, [(top + per_tile * step, per_tile, own, lat)])
        return carry

    lax.fori_loop(0, n_main, main_scatter, 0, unroll=4)

    sweep(a_buf, b_buf, 2, low + HALO - 2)
    outs = []
    for part in range(parts):
        begin = part * lon // parts
        size = (part + 1) * lon // parts - begin
        sweep(b_buf, a_buf, top + begin, top + begin + size)
        for half in range(2):
            copy = pltpu.make_async_copy(
                a_buf.at[half, pl.ds(top + begin, size), pl.ds(own, lat), :],
                out.at[pl.ds(begin, size), :, pl.ds(half * lanes, lanes)],
                out_sem.at[len(outs)],
            )
            copy.start()
            outs.append(copy)
    for copy in outs:
        copy.wait()


def exchange(
    n_lon, state, listed, counts,
    north, south, side, corner_n, corner_s, keys, offs,
    tiles, mine, strip, above, below, other, above_x, below_x, edges, lines, nooks, edge_sem, send_sem, recv_sem,
):
    lon, lat, _ = state.shape
    place, me = lax.axis_index("lon"), lax.axis_index("lat")
    east, west, across = lax.rem(place + 1, n_lon), lax.rem(place + n_lon - 1, n_lon), 1 - me
    others = [(west, me), (east, me), (place, across), (west, across), (east, across)]

    def device(spot):
        return {"lon": spot[0], "lat": spot[1]}

    loads = [
        pltpu.make_async_copy(state.at[pl.ds(row, HALO)], edges.at[which], edge_sem.at[which])
        for which, row in ((0, 0), (1, lon - HALO))
    ]
    for load in loads:
        load.start()
    barrier = pltpu.get_barrier_semaphore()
    for spot in others:
        pl.semaphore_signal(
            barrier, inc=1, device_id=device(spot), device_id_type=pl.DeviceIdType.MESH
        )
    pl.semaphore_wait(barrier, len(others))

    sent = []

    def send(source, target, spot):
        copy = pltpu.make_async_remote_copy(
            src_ref=source,
            dst_ref=target,
            send_sem=send_sem.at[len(sent)],
            recv_sem=recv_sem.at[len(sent)],
            device_id=device(spot),
            device_id_type=pl.DeviceIdType.MESH,
        )
        copy.start()
        sent.append(copy)

    for which, target, spot in ((0, south, others[0]), (1, north, others[1])):
        loads[which].wait()
        lines[which] = edges[which].astype(jnp.bfloat16)
        send(lines.at[which], target, spot)
    cut = pl.ds(pl.multiple_of(jnp.where(me == 0, lat - BLOCK, 0), BLOCK), BLOCK)
    for which, target, spot in ((0, corner_s, others[3]), (1, corner_n, others[4])):
        nooks[which] = edges[which, :, cut, :].reshape(nooks.shape[1:]).astype(jnp.bfloat16)
        send(nooks.at[which], target, spot)
    send(state.at[:, cut], side, others[2])

    numbers = listed[...]
    length = numbers.shape[1]
    active = lax.broadcasted_iota(jnp.int32, (1, length), 1) < counts[place]
    numbers = jnp.where(active, numbers, -1)
    rows = lax.shift_right_arithmetic(numbers, jnp.int32(lat.bit_length() - 1))
    spots = numbers & (lat - 1)

    def hot(number, size):
        same = lax.broadcasted_iota(jnp.int32, (size, length), 0) == number
        return jnp.where(same, 1.0, 0.0).astype(jnp.bfloat16)

    def marks(tile, position, size):
        return lax.dot_general(
            hot(tile, size), hot(position, TILE), (((1,), (1,)), ((), ())),
            preferred_element_type=jnp.float32,
        )

    n_main = lon * lat // TILE
    mine[...] = marks(
        lax.shift_right_arithmetic(numbers, jnp.int32(TILE.bit_length() - 1)), numbers & (TILE - 1), n_main
    )
    height = TILE // BLOCK
    reached = jnp.where(me == 0, lat - 2, 0)
    close = (spots >= reached) & (spots < reached + 2)
    strip_tile = jnp.where(
        close, lax.shift_right_arithmetic(rows, jnp.int32(height.bit_length() - 1)), -1
    )
    strip[...] = marks(strip_tile, (rows & (height - 1)) * BLOCK + (spots & (BLOCK - 1)), BLOCK)
    send(mine.at[pl.ds(0, BLOCK)], below, others[0])
    send(mine.at[pl.ds(n_main - BLOCK, BLOCK)], above, others[1])
    send(strip, below_x, others[3])
    send(strip, above_x, others[4])
    send(strip, other, others[2])
    for copy in sent:
        copy.wait()

    n_strip = lon // height
    lane = lax.broadcasted_iota(jnp.int32, (BLOCK, TILE), 1)
    from_n = pltpu.roll(above_x[...], BLOCK, 1)[n_strip - 1 : n_strip]
    from_s = pltpu.roll(below_x[...], BLOCK, 1)[0:1]
    lane = lane[0:1]
    tiles[0:1, :] = jnp.where(lane < BLOCK, from_n, jnp.where(lane < 2 * BLOCK, from_s, 0.0))
    tiles[1 : 1 + n_strip, :] = other[0:n_strip, :]
    near = 2 * lat
    tiles[1 + n_strip : 2 + n_strip, 0:near] = above[BLOCK - 1 : BLOCK, TILE - near :]
    tiles[1 + n_strip : 2 + n_strip, near:] = below[0:1, 0:near]
    filled = 2 + n_strip + n_main
    tiles[2 + n_strip : filled, :] = mine[...]
    size = tiles.shape[0]
    if filled < size:
        tiles[filled:, :] = jnp.zeros((size - filled, TILE), jnp.float32)
    marked = tiles[...]
    before = jnp.where(
        lax.broadcasted_iota(jnp.int32, (TILE, TILE), 0) < lax.broadcasted_iota(jnp.int32, (TILE, TILE), 1),
        1.0,
        0.0,
    ).astype(jnp.bfloat16)
    ranks = jnp.dot(marked.astype(jnp.bfloat16), before, preferred_element_type=jnp.float32)
    keys[...] = jnp.where(marked > 0.5, ranks, -1.0)
    counts = jnp.sum(marked, axis=1, keepdims=True)
    counts = jnp.floor((counts + (ALIGN - 1)) * (1.0 / ALIGN)) * ALIGN
    earlier = jnp.where(
        lax.broadcasted_iota(jnp.int32, (size, size), 1) < lax.broadcasted_iota(jnp.int32, (size, size), 0),
        1.0,
        0.0,
    ).astype(jnp.bfloat16)
    offs[...] = jnp.dot(
        earlier,
        jnp.broadcast_to(counts, (size, offs.shape[1])).astype(jnp.bfloat16),
        preferred_element_type=jnp.float32,
    ).astype(jnp.int32)


def local(n_lon, state_in, diffusion, conv_index, conv_count, w_first, w_hidden, w_last):
    lon, lat, feat = state_in.shape

    listed = conv_index.reshape(1, -1)
    anywhere = pl.BlockSpec(memory_space=pltpu.HBM)
    vmem = pl.BlockSpec(memory_space=pltpu.VMEM)
    smem = pl.BlockSpec(memory_space=pltpu.SMEM)
    shape = jax.ShapeDtypeStruct
    lines = shape((HALO, lat, feat), jnp.bfloat16)
    block = shape((HALO * BLOCK, feat), jnp.bfloat16)
    n_tiles = 2 + lon * BLOCK // TILE + lon * lat // TILE
    padded = -(-(n_tiles + 1) // 8) * 8
    few = pltpu.VMEM((BLOCK, TILE), jnp.float32)
    north, south, side, corner_n, corner_s, keys, offs = pl.pallas_call(
        functools.partial(exchange, n_lon),
        out_shape=(lines, lines, shape((lon, BLOCK, feat), jnp.float32), block, block)
        + (shape((padded, TILE), jnp.float32), shape((padded, LANES), jnp.int32)),
        in_specs=[anywhere, vmem, smem],
        out_specs=(anywhere,) * 5 + (vmem, vmem),
        scratch_shapes=[
            pltpu.VMEM((padded, TILE), jnp.float32),
            pltpu.VMEM((lon * lat // TILE, TILE), jnp.float32),
            few, few, few, few, few, few,
            pltpu.VMEM((2, HALO, lat, feat), jnp.float32),
            pltpu.VMEM((2, HALO, lat, feat), jnp.bfloat16),
            pltpu.VMEM((2, HALO * BLOCK, feat), jnp.bfloat16),
            pltpu.SemaphoreType.DMA((2,)),
            pltpu.SemaphoreType.DMA((10,)),
            pltpu.SemaphoreType.DMA((10,)),
        ],
        compiler_params=pltpu.CompilerParams(
            collective_id=0, has_side_effects=True, vmem_limit_bytes=60 * 1024 * 1024
        ),
    )(state_in, listed, conv_count[0, :, 0])
    room = -(-(n_tiles * TILE + TILE) // ROWS) * ROWS
    wide = lat + BLOCK + 2 * PAD
    buf = pltpu.VMEM((2, lon + 2 * HALO, wide, feat // 2), jnp.float32)
    hidden = w_first.shape[1]
    return pl.pallas_call(
        kernel,
        out_shape=jax.ShapeDtypeStruct(state_in.shape, jnp.float32),
        in_specs=[anywhere] * 6 + [vmem, vmem, smem] + [anywhere] * 3,
        out_specs=anywhere,
        scratch_shapes=[
            buf,
            buf,
            pltpu.VMEM((room, feat), jnp.bfloat16),
            pltpu.VMEM((ROWS, hidden), jnp.bfloat16),
            pltpu.VMEM((ROWS, hidden), jnp.bfloat16),
            pltpu.VMEM(w_first.shape, jnp.bfloat16),
            pltpu.VMEM(w_hidden.shape, jnp.bfloat16),
            pltpu.VMEM(w_last.shape, jnp.bfloat16),
            pltpu.VMEM((2,) + north.shape, jnp.bfloat16),
            pltpu.VMEM((2,) + corner_n.shape, jnp.bfloat16),
            pltpu.SemaphoreType.DMA((16,)),
            pltpu.SemaphoreType.DMA((3,)),
            pltpu.SemaphoreType.DMA((8,)),
        ],
        compiler_params=pltpu.CompilerParams(vmem_limit_bytes=60 * 1024 * 1024),
    )(
        state_in, north, south, side, corner_n, corner_s, diffusion[None], keys, offs,
        w_first, w_hidden, w_last,
    )


def solution(mesh):
    return jax.shard_map(
        functools.partial(local, mesh.shape["lon"]),
        mesh=mesh,
        in_specs=(
            P(("ens", "lon"), "lat", None),
            P(),
            P(("ens", "lon"), "lat", None),
            P("ens", None, "lat"),
            P(),
            P(),
            P(),
        ),
        out_specs=P(("ens", "lon"), "lat", None),
        check_vma=False,
    )
```
